768 devices in a mesh: dp: 16 (over y, core), expert: 48 (over z, x).
Axes of the slice: x: 4, y: 8, z: 12, core: 2. Of those that a mesh axis runs over, the one named last changes fastest.
Arguments:
- tokens: bfloat16 [6144, 8192], P('expert', 'dp'), may hold values from -6 to 6
- cotangent: bfloat16 [6144, 8192], P('expert', 'dp'), may hold values from -6 to 6
- routes: int32 [6144, 2], P('expert'), may hold values from 0 to 47, all different within a row; in each aligned block of 128 rows (0 to 127, 128 to 255, ...) at most 10 rows name the same one
- route_weight: float32 [6144, 2], P('expert'), may hold values from 0.25 to 1
- gate_dense: bfloat16 [18432, 8192], P('expert', 'dp'), may hold values from -0.0625 to 0.0625
- up_dense: bfloat16 [18432, 8192], P('expert', 'dp'), may hold values from -0.0625 to 0.0625
- down_dense: bfloat16 [18432, 8192], P('expert', 'dp'), may hold values from -0.3125 to 0.3125
- slice_map: int32 [18432], replicated, may hold values from 0 to 18431, as said below
Outputs:
- mixed: bfloat16 [6144, 8192], P('expert', 'dp')
- grad_gate: bfloat16 [18432, 8192], P('expert', 'dp')
- grad_up: bfloat16 [18432, 8192], P('expert', 'dp')
- grad_down: bfloat16 [18432, 8192], P('expert', 'dp')
The draws below stay inside these ranges and needn't reach their ends.
Inputs may be any that keep to these rules, and one draw needn't show every extreme that they name: `slice_map`: A permutation of the dense rows: value v puts a row at position v % 384 of expert v // 384; the 384 rows of each index of expert give exactly 8 rows to every expert. `routes`: each row names 2 different experts; the 128 rows of one device name each expert at most 10 times.
All inputs are finite; a program needn't handle non-finite values.
Results may differ from the reference program's by a relative error of at most 0.0058.
Values may be sent and summed in bfloat16 or wider, within the bound.
A program may use at most 32 MiB of HBM per device.

```python
import math
import jax
import jax.numpy as jnp
import numpy as np
from jax import lax

D = 8192
HID = 384
TOPK = 2
TOK = 128
EXPERTS = 48
CAP = 10
FFW = 18432
TOKENS = 6144


def draw_slice_map(key, part):
    key = jax.random.fold_in(key, 7)
    first, second = jax.random.split(key)
    group = HID // EXPERTS
    block_perm = jax.vmap(lambda k: jax.random.permutation(k, HID))(jax.random.split(first, EXPERTS))
    target = (block_perm // group).astype(jnp.int32)
    onehot = (target[:, :, None] == jnp.arange(EXPERTS, dtype=jnp.int32)[None, None, :]).astype(jnp.int32)
    ranks = jnp.sum((jnp.cumsum(onehot, axis=1) - onehot) * onehot, axis=2)
    position_perm = jax.vmap(lambda k: jax.random.permutation(k, HID))(jax.random.split(second, EXPERTS)).astype(jnp.int32)
    source = jnp.arange(EXPERTS, dtype=jnp.int32)[:, None]
    position = position_perm[target, source * group + ranks]
    return (target * HID + position).reshape(-1).astype(jnp.int32)


def levels(own_key, dims, pieces, low, largest):
    def one(axis_at, blocks):
        steps = jax.random.uniform(jax.random.fold_in(jax.random.fold_in(own_key, 6), axis_at), (blocks,), jnp.float32, low / len(pieces), largest / len(pieces))
        return jnp.repeat(jnp.exp(steps), dims[axis_at] // blocks).reshape((-1,) + (1,) * (len(dims) - axis_at - 1))

    gain = one(*pieces[0])
    for cut in pieces[1:]:
        gain = gain * one(*cut)
    return gain


def routed_block(rng, own, number, rows, count, top, most, lean):
    ranking = jax.random.permutation(rng, count)
    heavy_load, usual = portions_of(count, rows * top, most, lean, True), portions_of(count, rows * top, most, lean, False)
    places = jnp.arange(count)

    def named(lengths, rotation):
        used = int((lengths > 0).sum())
        fixed = max(1, used // 4)
        moved = fixed + (places - fixed + rotation * (used - fixed)) % max(1, count - fixed)
        return jnp.zeros((count,), jnp.int32).at[ranking[jnp.where(places < fixed, places, moved)]].set(jnp.asarray(lengths, jnp.int32))

    lengths = jnp.where(number % 4 == 0, named(heavy_load, number // 4), named(usual, number - number // 4 - 1))
    mixed = jax.random.permutation(jax.random.fold_in(own, 3), count)
    giver, sink = mixed[0:count // 2 * 2:2], mixed[1:count // 2 * 2:2]
    margin = jnp.minimum(lengths[giver] - 1, most - lengths[sink]) // 2
    margin = jnp.where((giver == ranking[0]) | (sink == ranking[0]) | (lengths[sink] == 0), 0, jnp.maximum(margin, 0))
    moved = jax.random.randint(jax.random.fold_in(own, 4), (count // 2,), 0, 1 << 20) % (margin + 1)
    lengths = lengths.at[giver].add(-moved).at[sink].add(moved)
    members = jnp.searchsorted(jnp.cumsum(lengths), jnp.arange(rows * top), side="right").astype(jnp.int32)
    grid = members.reshape(top, rows).T
    grid = grid[jax.random.permutation(jax.random.fold_in(own, 1), rows)]
    rotation = jax.random.randint(jax.random.fold_in(own, 2), (rows, 1), 0, top)
    return jnp.take_along_axis(grid, (jnp.arange(top)[None, :] + rotation) % top, axis=1)


def portions_of(amount, total, limit, lean, full):
    weights = [(1 << 20) // math.isqrt(standing ** lean) + 1 for standing in range(1, amount + 1)]
    largest = limit if full else min(limit, max(-(-total // amount), total * weights[0] // sum(weights)))
    least = 1 if total - largest >= amount - 1 else 0
    counts, rest = [largest] + [least] * (amount - 1), total - largest - least * (amount - 1)
    while rest > 0:
        candidates = [i for i in range(1, amount) if counts[i] < largest] or [i for i in range(1, amount) if counts[i] < limit]
        whole, budget = sum([weights[i] for i in candidates]), rest
        for i in candidates:
            addition = min(limit - counts[i], max(1, budget * weights[i] // whole), rest)
            counts[i] = counts[i] + addition
            rest = rest - addition
    return np.array(counts)


def scatter_about(stream_key, shape, scale, most, cuts=(), kind=jnp.bfloat16):
    factor_of = levels(stream_key, shape, cuts, -0.22, 0.18) if cuts else 1.0
    values = jax.random.normal(stream_key, shape, jnp.float32) * scale * factor_of
    return jnp.minimum(jnp.maximum(values, -most), most).astype(kind)


def setup_inputs(seed: int = 0) -> dict:
    keys = jax.random.split(jax.random.key(seed), 9)
    tokens = scatter_about(keys[0], (TOKENS, D), 1.0, 6.0, ((0, 48), (1, 16)))
    cotangent = scatter_about(keys[1], (TOKENS, D), 1.0, 6.0, ((0, 48), (1, 16)))
    routes_keys = jax.random.split(jax.random.fold_in(keys[2], 1), TOKENS // TOK)
    routes_turns = jax.random.permutation(jax.random.fold_in(keys[2], 3), TOKENS // TOK)
    routes = jax.vmap(lambda own, number: routed_block(jax.random.fold_in(keys[2], 2), own, number, TOK, EXPERTS, TOPK, CAP, 2))(routes_keys, routes_turns).reshape((TOKENS, TOPK))
    route_weight = jnp.clip(0.25 + 0.75 * jax.random.uniform(keys[3], (TOKENS, TOPK), jnp.float32) ** levels(keys[3], (TOKENS, TOPK), ((0, 48),), -0.2, 0.2), 0.25, 1.0)
    gate_dense = scatter_about(keys[4], (FFW, D), D ** -0.5, 0.0625, ((0, 48), (1, 16)))
    up_dense = scatter_about(keys[5], (FFW, D), D ** -0.5, 0.0625, ((0, 48), (1, 16)))
    down_dense = scatter_about(keys[6], (FFW, D), HID ** -0.5, 0.3125, ((0, 48), (1, 16)))
    slice_map = draw_slice_map(jax.random.fold_in(keys[8], 71), 0)
    return {"tokens": tokens, "cotangent": cotangent, "routes": routes, "route_weight": route_weight, "gate_dense": gate_dense, "up_dense": up_dense, "down_dense": down_dense, "slice_map": slice_map}


def reference(tokens, cotangent, routes, route_weight, gate_dense, up_dense, down_dense, slice_map):
    rows_cap = EXPERTS * CAP

    def regroup(dense):
        return jnp.zeros_like(dense).at[slice_map].set(dense).reshape(EXPERTS, HID, D)

    gate_e = regroup(gate_dense)
    up_e = regroup(up_dense)
    expert_down_weight = regroup(down_dense)
    flat = routes.reshape(-1)
    wflat = route_weight.reshape(-1)
    tok_of = (jnp.arange(TOKENS * TOPK, dtype=jnp.int32) // TOPK).astype(jnp.int32)

    def one(carry, expert_index):
        chosen = jnp.argsort((flat != expert_index).astype(jnp.int32), stable=True)[:rows_cap].astype(jnp.int32)
        valid = flat[chosen] == expert_index
        rowtok = tok_of[chosen]
        weight = jnp.where(valid, wflat[chosen], jnp.float32(0.0))
        inputs = jnp.where(valid[:, None], tokens[rowtok], jnp.zeros((), tokens.dtype)).astype(jnp.bfloat16)
        scaled_rows = (weight[:, None] * cotangent[rowtok].astype(jnp.float32)).astype(jnp.bfloat16)
        gmat = gate_e[expert_index]
        umat = up_e[expert_index]
        value_matrix = expert_down_weight[expert_index]
        gate = jnp.dot(inputs, gmat.T, preferred_element_type=jnp.float32)
        upval = jnp.dot(inputs, umat.T, preferred_element_type=jnp.float32)
        backward_pass = jnp.dot(scaled_rows, value_matrix.T, preferred_element_type=jnp.float32)
        sig = jax.nn.sigmoid(gate)
        hidden_state = (gate * sig * upval).astype(jnp.bfloat16)
        layer_output = jnp.dot(hidden_state, value_matrix, preferred_element_type=jnp.float32).astype(jnp.bfloat16)
        dgate = (backward_pass * upval * sig * (1.0 + gate * (1.0 - sig))).astype(jnp.bfloat16)
        dup = (backward_pass * gate * sig).astype(jnp.bfloat16)
        grad_g = jnp.dot(dgate.T, inputs, preferred_element_type=jnp.float32).astype(jnp.bfloat16)
        grad_u = jnp.dot(dup.T, inputs, preferred_element_type=jnp.float32).astype(jnp.bfloat16)
        grad_v = jnp.dot(hidden_state.T, scaled_rows, preferred_element_type=jnp.float32).astype(jnp.bfloat16)
        carry = carry.at[rowtok].add(weight[:, None] * layer_output.astype(jnp.float32))
        return carry, (grad_g, grad_u, grad_v)

    total, grads = lax.scan(one, jnp.zeros((TOKENS, D), jnp.float32), jnp.arange(EXPERTS, dtype=jnp.int32))

    def spread(grad):
        return grad.reshape(FFW, D)[slice_map]

    return total.astype(jnp.bfloat16), spread(grads[0]), spread(grads[1]), spread(grads[2])
```

```python
import functools

import jax
import jax.numpy as jnp
from jax import lax
from jax.experimental import pallas as pl
from jax.experimental.pallas import tpu as pltpu
from jax.sharding import PartitionSpec as P

BF = jnp.bfloat16
F32 = jnp.float32
NX = 4
LANE = 128
META = 16
BLK = 2 * LANE + META
GROUP = 8


def layer_kernel(
    Z,
    Y,
    meta_ref,
    tok_ref,
    cot_ref,
    wg_ref,
    wu_ref,
    wv_ref,
    ecol_ref,
    erow_ref,
    mixed_ref,
    gg_ref,
    gu_ref,
    gv_ref,
    TS,
    XB,
    WS,
    WB,
    VT,
    GS,
    PB,
    RB,
    HB,
    DD,
    ACC,
    OUT,
    MF,
    MB,
    MR,
    SS,
    SB,
    SL,
    SE,
    FS,
    FB,
    GO,
    GR,
    PT,
    x_send,
    x_recv,
    z_send,
    z_recv,
    s_send,
    s_recv,
    w_send,
    w_recv,
    p_send,
    p_recv,
    h_send,
    h_recv,
    m_send,
    m_recv,
    r_send,
    r_recv,
    f_send,
    f_recv,
    g_send,
    g_recv,
):
    E = Z * NX
    R = GROUP * E
    NH = Z // 2
    PAIRS = E // 2
    HALF = 2 * LANE
    dp = lax.axis_index("dp")
    ex = lax.axis_index("expert")
    y, c = dp // 2, dp % 2
    z, x = ex // NX, ex % NX
    other = 1 - c
    side = x // 2

    def dev(zz, xx, yy, cc):
        return (yy * 2 + cc, zz * NX + xx)

    z_next = dev((z + 1) % Z, x, y, c)
    z_prev = dev((z + Z - 1) % Z, x, y, c)
    sibling = dev(z, x, y, other)

    def remote(src, dst, send, recv, target):
        return pltpu.make_async_remote_copy(
            src_ref=src,
            dst_ref=dst,
            send_sem=send,
            recv_sem=recv,
            device_id=target,
            device_id_type=pl.DeviceIdType.MESH,
        )

    def wait_for(ref, sem):
        pltpu.make_async_copy(ref, ref, sem).wait()

    barrier = pltpu.get_barrier_semaphore()
    greeted = [z_next, z_prev]
    for dx in range(NX):
        for dc in range(2):
            if dx or dc:
                greeted.append(dev(z, (x + dx) % NX, y, (c + dc) % 2))
        for dy in range(1, Y):
            greeted.append(dev(z, (x + dx) % NX, (y + dy) % Y, c))
    for g in greeted:
        pl.semaphore_signal(barrier, inc=1, device_id=g, device_id_type=pl.DeviceIdType.MESH)

    for b in range(NX):
        lanes = slice(b * LANE, (b + 1) * LANE)
        TS[b, 0:LANE, :] = tok_ref[:, lanes]
        TS[b, LANE : LANE + META, :] = meta_ref[...]
        TS[b, LANE + META : BLK, :] = cot_ref[:, lanes]
    XB[0, x, c] = TS[x]
    pl.semaphore_wait(barrier, len(greeted))

    for dx in range(1, NX):
        to = (x + dx) % NX
        remote(
            TS.at[to], XB.at[0, x, c], x_send, x_recv.at[dx - 1], dev(z, to, y, c)
        ).start()

    ecol, erow = ecol_ref[...], erow_ref[...]
    same = ecol == erow
    i0 = lax.broadcasted_iota(jnp.int32, (R, R), 0)
    i1 = lax.broadcasted_iota(jnp.int32, (R, R), 1)
    rank_row = jnp.sum(jnp.where(same & (i0 < i1), 1.0, 0.0), axis=0, keepdims=True)
    rank_col = jnp.sum(jnp.where(same & (i1 < i0), 1.0, 0.0), axis=1, keepdims=True)
    pos_row = erow * GROUP + rank_row.astype(jnp.int32)
    pos_col = ecol * GROUP + rank_col.astype(jnp.int32)
    perm = jnp.where(i0 == pos_row, 1.0, 0.0).astype(BF)
    PT[...] = jnp.where(i1 == pos_col, 1.0, 0.0).astype(BF)
    for a, w_ref in enumerate((wg_ref, wu_ref, wv_ref)):
        for b in range(NX):
            lanes = slice(b * LANE, (b + 1) * LANE)
            WS[a, b] = jnp.dot(perm, w_ref[:, lanes], preferred_element_type=F32).astype(BF)
        for dx in range(NX):
            to = (x + dx) % NX
            copy = remote(
                WS.at[a, to],
                WB.at[a, x % 2, c],
                w_send.at[a, dx],
                w_recv.at[a, x % 2, c],
                dev(z, to, y, side),
            )
            if dx:
                copy.start()
            else:

                @pl.when(c == side)
                def _():
                    WB[a, x % 2, c] = WS[a, x]

                @pl.when(c != side)
                def _():
                    copy.start()

    ACC[...] = jnp.zeros_like(ACC)
    for way in range(2):
        for half in range(2):
            first = NH if way == half else NH - 1
            SB[way, half, first] = jnp.zeros((LANE, HALF), BF)

    def forward(s, tau):
        remote(
            XB.at[s, tau, c],
            XB.at[s + 1, tau, c],
            z_send.at[s],
            z_recv.at[s + 1, tau],
            z_next if tau < 2 else z_prev,
        ).start()

    def share(s, tau):
        remote(XB.at[s, tau, c], XB.at[s, tau, c], s_send.at[s], s_recv.at[s], sibling).start()

    for dx in range(1, NX):
        wait_for(XB.at[0, (x + NX - dx) % NX, c], x_recv.at[dx - 1])
    for tau in (0, 2, 1, 3):
        forward(0, tau)
    for tau in range(NX):
        share(0, tau)

    for a in range(3):
        for i in range(2):
            for cc in range(2):

                @pl.when(jnp.logical_not((2 * c + i == x) & (cc == c)))
                def _():
                    wait_for(WB.at[a, i, cc], w_recv.at[a, i, cc])

    for i in range(2):
        for cc in range(2):
            VT[cc * LANE : (cc + 1) * LANE, i * R : (i + 1) * R] = jnp.transpose(
                WB[2, i, cc].astype(F32)
            ).astype(BF)

    def arrive(s):
        for tau in (0, 2, 1, 3):
            wait_for(XB.at[s, tau, c], z_recv.at[s, tau])

            @pl.when(s < Z - 1)
            def _():
                forward(s, tau)

            share(s, tau)

    sub = lax.broadcasted_iota(jnp.int32, (16, LANE), 0) // 8

    def named(s, tau):
        rows = XB[s, tau, c, LANE : LANE + META, :].astype(F32)
        return [
            (jnp.broadcast_to(rows[k : k + 1, :], (16, LANE)) - sub.astype(F32)).astype(BF)
            for k in range(2)
        ]

    def owner_of(s, tau):
        return tau, (tau + s) % Y

    def project(s):
        wait_for(XB.at[s, :, other], s_recv.at[s])
        for h in range(2):
            taus = (2 * h, 2 * h + 1)

            def rows_of(first):
                return jnp.concatenate(
                    [
                        jnp.concatenate(
                            [XB[s, tau, cc, first : first + LANE, :] for cc in range(2)], axis=1
                        )
                        for tau in taus
                    ],
                    axis=0,
                )

            for first, arrays in ((0, (0, 1)), (LANE + META, (2,))):
                right = rows_of(first)
                for a in arrays:
                    for i in range(2):
                        left = jnp.concatenate([WB[a, i, 0], WB[a, i, 1]], axis=1)
                        GS[a * 2 + i] = lax.dot_general(
                            left,
                            right,
                            (((1,), (1,)), ((), ())),
                            preferred_element_type=F32,
                        ).astype(BF)
            for p, tau in enumerate(taus):
                lanes = slice(p * LANE, (p + 1) * LANE)
                who = named(s, tau)
                kept = [[jnp.zeros((16, LANE), BF) for _ in range(6)] for _ in range(2)]
                for m in range(PAIRS):
                    hits = [who[k] == jnp.asarray(2 * m, BF) for k in range(2)]
                    for q in range(6):
                        value = GS[q, 16 * m : 16 * m + 16, lanes]
                        for k in range(2):
                            kept[k][q] = jnp.where(hits[k], value, kept[k][q])
                for a in range(3):
                    for k in range(2):
                        parts = []
                        for i in range(2):
                            v = kept[k][a * 2 + i].astype(F32)
                            parts.append(v[0:8] + v[8:16])
                        PB[s, tau, a * 32 + k * 16 : a * 32 + k * 16 + 16, :] = jnp.concatenate(
                            parts, axis=0
                        ).astype(BF)
        for tau in range(NX):
            ox, oy = owner_of(s, tau)
            slot = ((x - ox + NX) % NX) * Y + (y - oy + Y) % Y

            @pl.when(slot != 0)
            def _():
                remote(
                    PB.at[s, tau],
                    RB.at[s // Y, slot - 1],
                    p_send.at[s],
                    p_recv.at[s // Y],
                    dev(z, ox, oy, c),
                ).start()

    def activate(s):
        wait_for(RB.at[s // Y], p_recv.at[s // Y])
        total = PB[s, x].astype(F32)
        for slot in range(NX * Y - 1):
            total = total + RB[s // Y, slot].astype(F32)
        meta = XB[s, x, c, LANE : LANE + META, :].astype(F32)
        for k in range(2):
            w = meta[2 + 3 * k : 3 + 3 * k] + meta[3 + 3 * k : 4 + 3 * k] + meta[4 + 3 * k : 5 + 3 * k]
            gate = total[k * 16 : k * 16 + 16]
            up = total[32 + k * 16 : 48 + k * 16]
            back = total[64 + k * 16 : 80 + k * 16] * w
            sig = 1.0 / (1.0 + jnp.exp(-gate))
            HB[s, x, k * 16 : k * 16 + 16, :] = (
                back * up * sig * (1.0 + gate * (1.0 - sig))
            ).astype(BF)
            HB[s, x, 32 + k * 16 : 48 + k * 16, :] = (back * gate * sig).astype(BF)
            HB[s, x, 64 + k * 16 : 80 + k * 16, :] = (w * (gate * sig * up)).astype(BF)
        for dx in range(NX):
            for dy in range(Y):
                if dx or dy:
                    remote(
                        HB.at[s, x],
                        HB.at[s, x],
                        h_send.at[s // Y],
                        h_recv.at[s, x],
                        dev(z, (x + dx) % NX, (y + dy) % Y, c),
                    ).start()

    def apply(s):
        for tau in range(NX):
            ox, oy = owner_of(s, tau)

            @pl.when(jnp.logical_not((ox == x) & (oy == y)))
            def _():
                wait_for(HB.at[s, tau], h_recv.at[s, tau])

        for tau in range(NX):
            lanes = slice(tau * LANE, (tau + 1) * LANE)
            who = named(s, tau)
            twice = []
            for a in range(3):
                for k in range(2):
                    v = HB[s, tau, a * 32 + k * 16 : a * 32 + k * 16 + 16, :].astype(F32)
                    for i in range(2):
                        v8 = v[8 * i : 8 * i + 8]
                        twice.append(jnp.concatenate([v8, v8], axis=0).astype(BF))
            zero = jnp.zeros((16, LANE), BF)
            for m in range(PAIRS):
                hits = [who[k] == jnp.asarray(2 * m, BF) for k in range(2)]
                for a in range(3):
                    for i in range(2):
                        DD[a, i * R + 16 * m : i * R + 16 * m + 16, lanes] = jnp.where(
                            hits[0],
                            twice[a * 4 + i],
                            jnp.where(hits[1], twice[a * 4 + 2 + i], zero),
                        )
        out = jnp.dot(VT[...], DD[2], preferred_element_type=F32)
        OUT[0] = out[0:LANE]
        OUT[1] = out[LANE : 2 * LANE]
        MB[s] = OUT[other].astype(BF)
        remote(MB.at[s], MR.at[s], m_send.at[s], m_recv.at[s], sibling).start()
        MF[s] = OUT[c]
        for first, arrays in ((0, (0, 1)), (LANE + META, (2,))):
            right = jnp.concatenate(
                [
                    jnp.concatenate(
                        [XB[s, tau, cc, first : first + LANE, :] for cc in range(2)], axis=1
                    )
                    for tau in range(NX)
                ],
                axis=0,
            )
            for a in arrays:
                ACC[a] += jnp.dot(DD[a], right, preferred_element_type=F32)

    def own_output(s, half):
        lanes = slice(half * HALF, (half + 1) * HALF)
        return MF[s, :, lanes] + MR[s, :, lanes].astype(F32)

    def pass_on(d):
        def flow(way, half):
            first = NH if way == half else NH - 1

            @pl.when(d < first)
            def _():
                wait_for(SB.at[way, half, d], r_recv.at[way, half, d])

            s = d if way == half else Z - d
            total = own_output(s, half) + SB[way, half, d].astype(F32)

            @pl.when(d == 1)
            def _():
                SL[way, half] = total
                remote(
                    SL.at[way, half],
                    SE.at[way, half],
                    r_send.at[way, half, 1],
                    r_recv.at[way, half, 0],
                    z_prev if way == 0 else z_next,
                ).start()

            @pl.when(d > 1)
            def _():
                SS[way, half, d] = total.astype(BF)
                remote(
                    SS.at[way, half, d],
                    SB.at[way, half, d - 1],
                    r_send.at[way, half, d],
                    r_recv.at[way, half, d - 1],
                    z_prev if way == 0 else z_next,
                ).start()

        flow(0, 0)
        flow(1, 1)

        @pl.when(d < NH)
        def _():
            flow(0, 1)
            flow(1, 0)

    def step(it, carry):
        @pl.when((it >= 1) & (it < Z))
        def _():
            arrive(it)

        @pl.when((it >= 2) & (it < Z + 2))
        def _():
            s = it - 2

            @pl.when((x + s) % Y == y)
            def _():
                activate(s)

        @pl.when((it >= 1) & (it < Z + 1))
        def _():
            project(it - 1)

        @pl.when((it >= 4 + NH) & (it < Z + 4))
        def _():
            s = it - 4
            wait_for(MR.at[s], m_recv.at[s])
            @pl.when(s > NH)
            def _():
                wait_for(MR.at[Z - s], m_recv.at[Z - s])
            pass_on(Z - s)

        @pl.when((it >= 3) & (it < Z + 3))
        def _():
            apply(it - 3)

        return carry

    lax.fori_loop(1, Z + 4, step, 0)

    for a in range(3):
        for i in range(2):
            for cc in range(2):
                GO[a, i, cc] = ACC[a, i * R : (i + 1) * R, cc * LANE : (cc + 1) * LANE].astype(BF)
        for i in range(2):
            for cc in range(2):
                mine = (2 * c + i == x) & (cc == c)

                @pl.when(jnp.logical_not(mine))
                def _():
                    remote(
                        GO.at[a, i, cc],
                        GR.at[a, x],
                        g_send.at[a, i, cc],
                        g_recv.at[a, x],
                        dev(z, 2 * c + i, y, cc),
                    ).start()

                @pl.when(mine)
                def _():
                    GR[a, x] = GO[a, i, cc]

    wait_for(MR.at[0], m_recv.at[0])
    for way in range(2):
        for half in range(2):
            wait_for(SE.at[way, half], r_recv.at[way, half, 0])
    for half in range(2):
        done = (
            own_output(0, half) + SE[0, half] + SE[1, half]
        ).astype(BF)
        for p in range(2):
            FS[2 * half + p] = done[:, p * LANE : (p + 1) * LANE]
    for dx in range(1, NX):
        to = (x + dx) % NX
        remote(FS.at[to], FB.at[x], f_send.at[dx - 1], f_recv.at[dx - 1], dev(z, to, y, c)).start()
    FB[x] = FS[x]
    for dx in range(1, NX):
        wait_for(FB.at[(x + NX - dx) % NX], f_recv.at[dx - 1])
    for b in range(NX):
        mixed_ref[:, b * LANE : (b + 1) * LANE] = jnp.transpose(FB[b].astype(F32)).astype(BF)

    for a, out_ref in enumerate((gg_ref, gu_ref, gv_ref)):
        for dx in range(NX):
            frm = (x + dx) % NX
            if dx:
                wait_for(GR.at[a, frm], g_recv.at[a, frm])
            else:

                @pl.when(c != side)
                def _():
                    wait_for(GR.at[a, frm], g_recv.at[a, frm])

        for b in range(NX):
            out_ref[:, b * LANE : (b + 1) * LANE] = jnp.dot(
                PT[...], GR[a, b], preferred_element_type=F32
            ).astype(BF)

    wait_for(TS.at[0 : NX - 1], x_send)
    for s in range(Z):
        if s < Z - 1:
            wait_for(XB.at[s, :, c], z_send.at[s])
        wait_for(XB.at[s, :, c], s_send.at[s])
        wait_for(MR.at[s], m_send.at[s])
        owned = (x + s) % Y == y

        @pl.when(owned)
        def _():
            wait_for(PB.at[s, 0 : NX - 1], p_send.at[s])
            wait_for(RB.at[s // Y], h_send.at[s // Y])

        @pl.when(jnp.logical_not(owned))
        def _():
            wait_for(PB.at[s], p_send.at[s])

    for a in range(3):
        for dx in range(NX):
            if dx:
                wait_for(WS.at[a, 0], w_send.at[a, dx])
            else:

                @pl.when(c != side)
                def _():
                    wait_for(WS.at[a, 0], w_send.at[a, 0])

        for i in range(2):
            for cc in range(2):

                @pl.when(jnp.logical_not((2 * c + i == x) & (cc == c)))
                def _():
                    wait_for(GO.at[a, i, cc], g_send.at[a, i, cc])

    for dx in range(1, NX):
        wait_for(FS.at[0], f_send.at[dx - 1])
    for way in range(2):
        for half in range(2):
            first = NH if way == half else NH - 1
            wait_for(SL.at[way, half], r_send.at[way, half, 1])
            for d in range(2, first + 1):
                wait_for(SS.at[way, half, d], r_send.at[way, half, d])


def local(Z, Y, tokens, cotangent, routes, route_weight, gate_dense, up_dense, down_dense, slice_map):
    rows, width = gate_dense.shape
    E = Z * NX
    here = lax.axis_index("expert")
    own = lax.dynamic_slice_in_dim(slice_map, here * rows, rows) // rows
    high = lax.reduce_precision(route_weight, 8, 7)
    rest = route_weight - high
    mid = lax.reduce_precision(rest, 8, 7)
    low = rest - mid
    pieces = [routes.astype(F32)] + [
        jnp.stack([high[:, k], mid[:, k], low[:, k]], axis=1) for k in range(2)
    ]
    meta = jnp.concatenate(pieces + [jnp.zeros((LANE, META - 8), F32)], axis=1).T.astype(BF)
    dma = pltpu.SemaphoreType.DMA
    NH = Z // 2
    scratch = [
        pltpu.VMEM((NX, BLK, LANE), BF),
        pltpu.VMEM((Z, NX, 2, BLK, LANE), BF),
        pltpu.VMEM((3, NX, rows, LANE), BF),
        pltpu.VMEM((3, 2, 2, rows, LANE), BF),
        pltpu.VMEM((2 * LANE, 2 * rows), BF),
        pltpu.VMEM((6, rows, 2 * LANE), BF),
        pltpu.VMEM((Z, NX, 96, LANE), BF),
        pltpu.VMEM((-(-Z // Y), NX * Y - 1, 96, LANE), BF),
        pltpu.VMEM((Z, NX, 96, LANE), BF),
        pltpu.VMEM((3, 2 * rows, 4 * LANE), BF),
        pltpu.VMEM((3, 2 * rows, 2 * LANE), F32),
        pltpu.VMEM((2, LANE, 4 * LANE), F32),
        pltpu.VMEM((Z, LANE, 4 * LANE), F32),
        pltpu.VMEM((Z, LANE, 4 * LANE), BF),
        pltpu.VMEM((Z, LANE, 4 * LANE), BF),
        pltpu.VMEM((2, 2, NH + 1, LANE, 2 * LANE), BF),
        pltpu.VMEM((2, 2, NH + 1, LANE, 2 * LANE), BF),
        pltpu.VMEM((2, 2, LANE, 2 * LANE), F32),
        pltpu.VMEM((2, 2, LANE, 2 * LANE), F32),
        pltpu.VMEM((NX, LANE, LANE), BF),
        pltpu.VMEM((NX, LANE, LANE), BF),
        pltpu.VMEM((3, 2, 2, rows, LANE), BF),
        pltpu.VMEM((3, NX, rows, LANE), BF),
        pltpu.VMEM((rows, rows), BF),
        dma,
        dma((NX - 1,)),
        dma((Z,)),
        dma((Z, NX)),
        dma((Z,)),
        dma((Z,)),
        dma((3, NX)),
        dma((3, 2, 2)),
        dma((Z,)),
        dma((-(-Z // Y),)),
        dma((-(-Z // Y),)),
        dma((Z, NX)),
        dma((Z,)),
        dma((Z,)),
        dma((2, 2, NH + 1)),
        dma((2, 2, NH + 1)),
        dma((NX - 1,)),
        dma((NX - 1,)),
        dma((3, 2, 2)),
        dma((3, NX)),
    ]
    vmem = pl.BlockSpec(memory_space=pltpu.VMEM)
    return pl.pallas_call(
        functools.partial(layer_kernel, Z, Y),
        out_shape=(
            jax.ShapeDtypeStruct(tokens.shape, BF),
            jax.ShapeDtypeStruct(gate_dense.shape, BF),
            jax.ShapeDtypeStruct(gate_dense.shape, BF),
            jax.ShapeDtypeStruct(gate_dense.shape, BF),
        ),
        in_specs=[vmem] * 8,
        out_specs=(vmem,) * 4,
        scratch_shapes=scratch,
        compiler_params=pltpu.CompilerParams(
            collective_id=0, has_side_effects=True, vmem_limit_bytes=52 * 1024 * 1024
        ),
    )(
        meta,
        tokens,
        cotangent,
        gate_dense,
        up_dense,
        down_dense,
        own.reshape(rows, 1),
        own.reshape(1, rows),
    )


def solution(mesh):
    Y = mesh.shape["dp"] // 2
    Z = mesh.shape["expert"] // NX
    return jax.shard_map(
        functools.partial(local, Z, Y),
        mesh=mesh,
        in_specs=(
            P("expert", "dp"),
            P("expert", "dp"),
            P("expert", None),
            P("expert", None),
            P("expert", "dp"),
            P("expert", "dp"),
            P("expert", "dp"),
            P(),
        ),
        out_specs=(P("expert", "dp"), P("expert", "dp"), P("expert", "dp"), P("expert", "dp")),
        check_vma=False,
    )
```

```python
import functools

import jax
import jax.numpy as jnp
from jax import lax
from jax.experimental import pallas as pl
from jax.experimental.pallas import tpu as pltpu
from jax.sharding import PartitionSpec as P

BF = jnp.bfloat16
F32 = jnp.float32
NX = 4
LANE = 128
META = 16
BLK = 2 * LANE + META
GROUP = 8


def layer_kernel(
    Z,
    Y,
    meta_ref,
    tok_ref,
    cot_ref,
    wg_ref,
    wu_ref,
    wv_ref,
    ecol_ref,
    erow_ref,
    mixed_ref,
    gg_ref,
    gu_ref,
    gv_ref,
    TS,
    XB,
    WS,
    WB,
    VT,
    GS,
    PB,
    RX,
    YS,
    YR,
    HB,
    DD,
    ACC,
    OUT,
    MF,
    MB,
    MR,
    SS,
    SB,
    SL,
    SE,
    FS,
    FB,
    GO,
    GR,
    PT,
    x_send,
    x_recv,
    z_send,
    z_recv,
    s_send,
    s_recv,
    w_send,
    w_recv,
    p_send,
    p_recv,
    y_send,
    y_recv,
    h_send,
    h_recv,
    m_send,
    m_recv,
    r_send,
    r_recv,
    f_send,
    f_recv,
    g_send,
    g_recv,
):
    E = Z * NX
    R = GROUP * E
    NH = Z // 2
    PAIRS = E // 2
    HALF = 2 * LANE
    dp = lax.axis_index("dp")
    ex = lax.axis_index("expert")
    y, c = dp // 2, dp % 2
    z, x = ex // NX, ex % NX
    other = 1 - c
    side = x // 2

    def dev(zz, xx, yy, cc):
        return (yy * 2 + cc, zz * NX + xx)

    z_next = dev((z + 1) % Z, x, y, c)
    z_prev = dev((z + Z - 1) % Z, x, y, c)
    sibling = dev(z, x, y, other)

    def remote(src, dst, send, recv, target):
        return pltpu.make_async_remote_copy(
            src_ref=src,
            dst_ref=dst,
            send_sem=send,
            recv_sem=recv,
            device_id=target,
            device_id_type=pl.DeviceIdType.MESH,
        )

    def wait_for(ref, sem):
        pltpu.make_async_copy(ref, ref, sem).wait()

    barrier = pltpu.get_barrier_semaphore()
    greeted = [z_next, z_prev]
    for dx in range(NX):
        for dc in range(2):
            if dx or dc:
                greeted.append(dev(z, (x + dx) % NX, y, (c + dc) % 2))
    for dy in range(1, Y):
        greeted.append(dev(z, x, (y + dy) % Y, c))
    for g in greeted:
        pl.semaphore_signal(barrier, inc=1, device_id=g, device_id_type=pl.DeviceIdType.MESH)

    for b in range(NX):
        lanes = slice(b * LANE, (b + 1) * LANE)
        TS[b, 0:LANE, :] = tok_ref[:, lanes]
        TS[b, LANE : LANE + META, :] = meta_ref[...]
        TS[b, LANE + META : BLK, :] = cot_ref[:, lanes]
    XB[0, x, c] = TS[x]
    pl.semaphore_wait(barrier, len(greeted))

    for dx in range(1, NX):
        to = (x + dx) % NX
        remote(
            TS.at[to], XB.at[0, x, c], x_send, x_recv.at[dx - 1], dev(z, to, y, c)
        ).start()

    ecol, erow = ecol_ref[...], erow_ref[...]
    same = ecol == erow
    i0 = lax.broadcasted_iota(jnp.int32, (R, R), 0)
    i1 = lax.broadcasted_iota(jnp.int32, (R, R), 1)
    rank_row = jnp.sum(jnp.where(same & (i0 < i1), 1.0, 0.0), axis=0, keepdims=True)
    rank_col = jnp.sum(jnp.where(same & (i1 < i0), 1.0, 0.0), axis=1, keepdims=True)
    pos_row = erow * GROUP + rank_row.astype(jnp.int32)
    pos_col = ecol * GROUP + rank_col.astype(jnp.int32)
    perm = jnp.where(i0 == pos_row, 1.0, 0.0).astype(BF)
    PT[...] = jnp.where(i1 == pos_col, 1.0, 0.0).astype(BF)
    for a, w_ref in enumerate((wg_ref, wu_ref, wv_ref)):
        for b in range(NX):
            lanes = slice(b * LANE, (b + 1) * LANE)
            WS[a, b] = jnp.dot(perm, w_ref[:, lanes], preferred_element_type=F32).astype(BF)
        for dx in range(NX):
            to = (x + dx) % NX
            copy = remote(
                WS.at[a, to],
                WB.at[a, x % 2, c],
                w_send.at[a, dx],
                w_recv.at[a, x % 2, c],
                dev(z, to, y, side),
            )
            if dx:
                copy.start()
            else:

                @pl.when(c == side)
                def _():
                    WB[a, x % 2, c] = WS[a, x]

                @pl.when(c != side)
                def _():
                    copy.start()

    ACC[...] = jnp.zeros_like(ACC)
    for way in range(2):
        for half in range(2):
            first = NH if way == half else NH - 1
            SB[way, half, first] = jnp.zeros((LANE, HALF), BF)

    def forward(s, tau):
        remote(
            XB.at[s, tau, c],
            XB.at[s + 1, tau, c],
            z_send.at[s],
            z_recv.at[s + 1, tau],
            z_next if tau < 2 else z_prev,
        ).start()

    def share(s, tau):
        remote(XB.at[s, tau, c], XB.at[s, tau, c], s_send.at[s], s_recv.at[s], sibling).start()

    for dx in range(1, NX):
        wait_for(XB.at[0, (x + NX - dx) % NX, c], x_recv.at[dx - 1])
    for tau in (0, 2, 1, 3):
        forward(0, tau)
    for tau in range(NX):
        share(0, tau)

    for a in range(3):
        for i in range(2):
            for cc in range(2):

                @pl.when(jnp.logical_not((2 * c + i == x) & (cc == c)))
                def _():
                    wait_for(WB.at[a, i, cc], w_recv.at[a, i, cc])

    for i in range(2):
        for cc in range(2):
            VT[cc * LANE : (cc + 1) * LANE, i * R : (i + 1) * R] = jnp.transpose(
                WB[2, i, cc].astype(F32)
            ).astype(BF)

    def arrive(s):
        for tau in (0, 2, 1, 3):
            wait_for(XB.at[s, tau, c], z_recv.at[s, tau])

            @pl.when(s < Z - 1)
            def _():
                forward(s, tau)

            share(s, tau)

    sub = lax.broadcasted_iota(jnp.int32, (16, LANE), 0) // 8

    def named(s, tau):
        rows = XB[s, tau, c, LANE : LANE + META, :].astype(F32)
        return [jnp.broadcast_to(rows[k : k + 1, :], (16, LANE)) for k in range(2)]

    def project(s):
        wait_for(XB.at[s, :, other], s_recv.at[s])
        for h in range(2):
            taus = (2 * h, 2 * h + 1)

            def rows_of(first):
                return jnp.concatenate(
                    [
                        jnp.concatenate(
                            [XB[s, tau, cc, first : first + LANE, :] for cc in range(2)], axis=1
                        )
                        for tau in taus
                    ],
                    axis=0,
                )

            for first, arrays in ((0, (0, 1)), (LANE + META, (2,))):
                right = rows_of(first)
                for a in arrays:
                    for i in range(2):
                        left = jnp.concatenate([WB[a, i, 0], WB[a, i, 1]], axis=1)
                        GS[a * 2 + i] = lax.dot_general(
                            left,
                            right,
                            (((1,), (1,)), ((), ())),
                            preferred_element_type=F32,
                        )
            for p, tau in enumerate(taus):
                lanes = slice(p * LANE, (p + 1) * LANE)
                who = [w[0:8] for w in named(s, tau)]
                kept = [[jnp.zeros((8, LANE), F32) for _ in range(6)] for _ in range(2)]
                for e in range(E):
                    hits = [who[k] == float(e) for k in range(2)]
                    for q in range(6):
                        value = GS[q, 8 * e : 8 * e + 8, lanes]
                        for k in range(2):
                            kept[k][q] = jnp.where(hits[k], value, kept[k][q])
                for a in range(3):
                    for k in range(2):
                        for i in range(2):
                            row = a * 32 + k * 16 + i * 8
                            PB[s, tau, row : row + 8, :] = kept[k][a * 2 + i]
        for dx in range(1, NX):
            to = (x + dx) % NX
            remote(
                PB.at[s, to], RX.at[s, dx - 1], p_send.at[s], p_recv.at[s], dev(z, to, y, c)
            ).start()

    def sum_x(s):
        wait_for(RX.at[s], p_recv.at[s])
        YS[s] = (PB[s, x] + RX[s, 0] + RX[s, 1] + RX[s, 2]).astype(BF)
        for dy in range(1, Y):
            remote(
                YS.at[s], YR.at[s, dy - 1], y_send.at[s], y_recv.at[s], dev(z, x, (y + dy) % Y, c)
            ).start()

    def activate(s):
        wait_for(YR.at[s], y_recv.at[s])
        total = YS[s].astype(F32)
        for slot in range(Y - 1):
            total = total + YR[s, slot].astype(F32)
        meta = XB[s, x, c, LANE : LANE + META, :].astype(F32)
        for k in range(2):
            w = meta[2 + 3 * k : 3 + 3 * k] + meta[3 + 3 * k : 4 + 3 * k] + meta[4 + 3 * k : 5 + 3 * k]
            gate = total[k * 16 : k * 16 + 16]
            up = total[32 + k * 16 : 48 + k * 16]
            back = total[64 + k * 16 : 80 + k * 16] * w
            sig = 1.0 / (1.0 + jnp.exp(-gate))
            HB[s, x, k * 16 : k * 16 + 16, :] = (
                back * up * sig * (1.0 + gate * (1.0 - sig))
            ).astype(BF)
            HB[s, x, 32 + k * 16 : 48 + k * 16, :] = (back * gate * sig).astype(BF)
            HB[s, x, 64 + k * 16 : 80 + k * 16, :] = (w * (gate * sig * up)).astype(BF)
        for dx in range(1, NX):
            remote(
                HB.at[s, x], HB.at[s, x], h_send.at[s], h_recv.at[s, x], dev(z, (x + dx) % NX, y, c)
            ).start()

    def apply(s):
        for tau in range(NX):

            @pl.when(tau != x)
            def _():
                wait_for(HB.at[s, tau], h_recv.at[s, tau])

        for tau in range(NX):
            lanes = slice(tau * LANE, (tau + 1) * LANE)
            who = [(w - sub.astype(F32)).astype(BF) for w in named(s, tau)]
            twice = []
            for a in range(3):
                for k in range(2):
                    v = HB[s, tau, a * 32 + k * 16 : a * 32 + k * 16 + 16, :].astype(F32)
                    for i in range(2):
                        v8 = v[8 * i : 8 * i + 8]
                        twice.append(jnp.concatenate([v8, v8], axis=0).astype(BF))
            zero = jnp.zeros((16, LANE), BF)
            for m in range(PAIRS):
                hits = [who[k] == jnp.asarray(2 * m, BF) for k in range(2)]
                for a in range(3):
                    for i in range(2):
                        DD[a, i * R + 16 * m : i * R + 16 * m + 16, lanes] = jnp.where(
                            hits[0],
                            twice[a * 4 + i],
                            jnp.where(hits[1], twice[a * 4 + 2 + i], zero),
                        )
        out = jnp.dot(VT[...], DD[2], preferred_element_type=F32)
        OUT[0] = out[0:LANE]
        OUT[1] = out[LANE : 2 * LANE]
        MB[s] = OUT[other].astype(BF)
        remote(MB.at[s], MR.at[s], m_send.at[s], m_recv.at[s], sibling).start()
        MF[s] = OUT[c]
        for first, arrays in ((0, (0, 1)), (LANE + META, (2,))):
            right = jnp.concatenate(
                [
                    jnp.concatenate(
                        [XB[s, tau, cc, first : first + LANE, :] for cc in range(2)], axis=1
                    )
                    for tau in range(NX)
                ],
                axis=0,
            )
            for a in arrays:
                ACC[a] += jnp.dot(DD[a], right, preferred_element_type=F32)

    def own_output(s, half):
        lanes = slice(half * HALF, (half + 1) * HALF)
        return MF[s, :, lanes] + MR[s, :, lanes].astype(F32)

    def pass_on(d):
        def flow(way, half):
            first = NH if way == half else NH - 1

            @pl.when(d < first)
            def _():
                wait_for(SB.at[way, half, d], r_recv.at[way, half, d])

            s = d if way == half else Z - d
            total = own_output(s, half) + SB[way, half, d].astype(F32)

            @pl.when(d == 1)
            def _():
                SL[way, half] = total
                remote(
                    SL.at[way, half],
                    SE.at[way, half],
                    r_send.at[way, half, 1],
                    r_recv.at[way, half, 0],
                    z_prev if way == 0 else z_next,
                ).start()

            @pl.when(d > 1)
            def _():
                SS[way, half, d] = total.astype(BF)
                remote(
                    SS.at[way, half, d],
                    SB.at[way, half, d - 1],
                    r_send.at[way, half, d],
                    r_recv.at[way, half, d - 1],
                    z_prev if way == 0 else z_next,
                ).start()

        flow(0, 0)
        flow(1, 1)

        @pl.when(d < NH)
        def _():
            flow(0, 1)
            flow(1, 0)

    def step(it, carry):
        @pl.when((it >= 1) & (it < Z))
        def _():
            arrive(it)

        @pl.when((it >= 1) & (it < Z + 1))
        def _():
            project(it - 1)

        @pl.when((it >= 2) & (it < Z + 2))
        def _():
            sum_x(it - 2)

        @pl.when((it >= 3) & (it < Z + 3))
        def _():
            activate(it - 3)

        @pl.when((it >= 5 + NH) & (it < Z + 5))
        def _():
            s = it - 5
            wait_for(MR.at[s], m_recv.at[s])

            @pl.when(s > NH)
            def _():
                wait_for(MR.at[Z - s], m_recv.at[Z - s])

            pass_on(Z - s)

        @pl.when((it >= 4) & (it < Z + 4))
        def _():
            apply(it - 4)

        return carry

    lax.fori_loop(1, Z + 5, step, 0)

    for a in range(3):
        for i in range(2):
            for cc in range(2):
                GO[a, i, cc] = ACC[a, i * R : (i + 1) * R, cc * LANE : (cc + 1) * LANE].astype(BF)
        for i in range(2):
            for cc in range(2):
                mine = (2 * c + i == x) & (cc == c)

                @pl.when(jnp.logical_not(mine))
                def _():
                    remote(
                        GO.at[a, i, cc],
                        GR.at[a, x],
                        g_send.at[a, i, cc],
                        g_recv.at[a, x],
                        dev(z, 2 * c + i, y, cc),
                    ).start()

                @pl.when(mine)
                def _():
                    GR[a, x] = GO[a, i, cc]

    wait_for(MR.at[0], m_recv.at[0])
    for way in range(2):
        for half in range(2):
            wait_for(SE.at[way, half], r_recv.at[way, half, 0])
    for half in range(2):
        done = (
            own_output(0, half) + SE[0, half] + SE[1, half]
        ).astype(BF)
        for p in range(2):
            FS[2 * half + p] = done[:, p * LANE : (p + 1) * LANE]
    for dx in range(1, NX):
        to = (x + dx) % NX
        remote(FS.at[to], FB.at[x], f_send.at[dx - 1], f_recv.at[dx - 1], dev(z, to, y, c)).start()
    FB[x] = FS[x]
    for dx in range(1, NX):
        wait_for(FB.at[(x + NX - dx) % NX], f_recv.at[dx - 1])
    for b in range(NX):
        mixed_ref[:, b * LANE : (b + 1) * LANE] = jnp.transpose(FB[b].astype(F32)).astype(BF)

    for a, out_ref in enumerate((gg_ref, gu_ref, gv_ref)):
        for dx in range(NX):
            frm = (x + dx) % NX
            if dx:
                wait_for(GR.at[a, frm], g_recv.at[a, frm])
            else:

                @pl.when(c != side)
                def _():
                    wait_for(GR.at[a, frm], g_recv.at[a, frm])

        for b in range(NX):
            out_ref[:, b * LANE : (b + 1) * LANE] = jnp.dot(
                PT[...], GR[a, b], preferred_element_type=F32
            ).astype(BF)

    wait_for(TS.at[0 : NX - 1], x_send)
    for s in range(Z):
        if s < Z - 1:
            wait_for(XB.at[s, :, c], z_send.at[s])
        wait_for(XB.at[s, :, c], s_send.at[s])
        wait_for(MR.at[s], m_send.at[s])
        wait_for(RX.at[s], p_send.at[s])
        wait_for(YR.at[s], y_send.at[s])
        wait_for(HB.at[s, 0 : NX - 1], h_send.at[s])
    for a in range(3):
        for dx in range(NX):
            if dx:
                wait_for(WS.at[a, 0], w_send.at[a, dx])
            else:

                @pl.when(c != side)
                def _():
                    wait_for(WS.at[a, 0], w_send.at[a, 0])

        for i in range(2):
            for cc in range(2):

                @pl.when(jnp.logical_not((2 * c + i == x) & (cc == c)))
                def _():
                    wait_for(GO.at[a, i, cc], g_send.at[a, i, cc])

    for dx in range(1, NX):
        wait_for(FS.at[0], f_send.at[dx - 1])
    for way in range(2):
        for half in range(2):
            first = NH if way == half else NH - 1
            wait_for(SL.at[way, half], r_send.at[way, half, 1])
            for d in range(2, first + 1):
                wait_for(SS.at[way, half, d], r_send.at[way, half, d])


def local(Z, Y, tokens, cotangent, routes, route_weight, gate_dense, up_dense, down_dense, slice_map):
    rows, width = gate_dense.shape
    E = Z * NX
    here = lax.axis_index("expert")
    own = lax.dynamic_slice_in_dim(slice_map, here * rows, rows) // rows
    high = lax.reduce_precision(route_weight, 8, 7)
    rest = route_weight - high
    mid = lax.reduce_precision(rest, 8, 7)
    low = rest - mid
    pieces = [routes.astype(F32)] + [
        jnp.stack([high[:, k], mid[:, k], low[:, k]], axis=1) for k in range(2)
    ]
    meta = jnp.concatenate(pieces + [jnp.zeros((LANE, META - 8), F32)], axis=1).T.astype(BF)
    dma = pltpu.SemaphoreType.DMA
    NH = Z // 2
    scratch = [
        pltpu.VMEM((NX, BLK, LANE), BF),
        pltpu.VMEM((Z, NX, 2, BLK, LANE), BF),
        pltpu.VMEM((3, NX, rows, LANE), BF),
        pltpu.VMEM((3, 2, 2, rows, LANE), BF),
        pltpu.VMEM((2 * LANE, 2 * rows), BF),
        pltpu.VMEM((6, rows, 2 * LANE), F32),
        pltpu.VMEM((Z, NX, 96, LANE), F32),
        pltpu.VMEM((Z, NX - 1, 96, LANE), F32),
        pltpu.VMEM((Z, 96, LANE), BF),
        pltpu.VMEM((Z, Y - 1, 96, LANE), BF),
        pltpu.VMEM((Z, NX, 96, LANE), BF),
        pltpu.VMEM((3, 2 * rows, 4 * LANE), BF),
        pltpu.VMEM((3, 2 * rows, 2 * LANE), F32),
        pltpu.VMEM((2, LANE, 4 * LANE), F32),
        pltpu.VMEM((Z, LANE, 4 * LANE), F32),
        pltpu.VMEM((Z, LANE, 4 * LANE), BF),
        pltpu.VMEM((Z, LANE, 4 * LANE), BF),
        pltpu.VMEM((2, 2, NH + 1, LANE, 2 * LANE), BF),
        pltpu.VMEM((2, 2, NH + 1, LANE, 2 * LANE), BF),
        pltpu.VMEM((2, 2, LANE, 2 * LANE), F32),
        pltpu.VMEM((2, 2, LANE, 2 * LANE), F32),
        pltpu.VMEM((NX, LANE, LANE), BF),
        pltpu.VMEM((NX, LANE, LANE), BF),
        pltpu.VMEM((3, 2, 2, rows, LANE), BF),
        pltpu.VMEM((3, NX, rows, LANE), BF),
        pltpu.VMEM((rows, rows), BF),
        dma,
        dma((NX - 1,)),
        dma((Z,)),
        dma((Z, NX)),
        dma((Z,)),
        dma((Z,)),
        dma((3, NX)),
        dma((3, 2, 2)),
        dma((Z,)),
        dma((Z,)),
        dma((Z,)),
        dma((Z,)),
        dma((Z,)),
        dma((Z, NX)),
        dma((Z,)),
        dma((Z,)),
        dma((2, 2, NH + 1)),
        dma((2, 2, NH + 1)),
        dma((NX - 1,)),
        dma((NX - 1,)),
        dma((3, 2, 2)),
        dma((3, NX)),
    ]
    vmem = pl.BlockSpec(memory_space=pltpu.VMEM)
    return pl.pallas_call(
        functools.partial(layer_kernel, Z, Y),
        out_shape=(
            jax.ShapeDtypeStruct(tokens.shape, BF),
            jax.ShapeDtypeStruct(gate_dense.shape, BF),
            jax.ShapeDtypeStruct(gate_dense.shape, BF),
            jax.ShapeDtypeStruct(gate_dense.shape, BF),
        ),
        in_specs=[vmem] * 8,
        out_specs=(vmem,) * 4,
        scratch_shapes=scratch,
        compiler_params=pltpu.CompilerParams(
            collective_id=0, has_side_effects=True, vmem_limit_bytes=52 * 1024 * 1024
        ),
    )(
        meta,
        tokens,
        cotangent,
        gate_dense,
        up_dense,
        down_dense,
        own.reshape(rows, 1),
        own.reshape(1, rows),
    )


def solution(mesh):
    Y = mesh.shape["dp"] // 2
    Z = mesh.shape["expert"] // NX
    return jax.shard_map(
        functools.partial(local, Z, Y),
        mesh=mesh,
        in_specs=(
            P("expert", "dp"),
            P("expert", "dp"),
            P("expert", None),
            P("expert", None),
            P("expert", "dp"),
            P("expert", "dp"),
            P("expert", "dp"),
            P(),
        ),
        out_specs=(P("expert", "dp"), P("expert", "dp"), P("expert", "dp"), P("expert", "dp")),
        check_vma=False,
    )
```

```python
import functools

import jax
import jax.numpy as jnp
from jax import lax
from jax.experimental import pallas as pl
from jax.experimental.pallas import tpu as pltpu
from jax.sharding import PartitionSpec as P

BF = jnp.bfloat16
F32 = jnp.float32
NX = 4
LANE = 128
META = 16
BLK = 2 * LANE + META
GROUP = 8


def layer_kernel(
    Z,
    Y,
    meta_ref,
    tok_ref,
    cot_ref,
    wg_ref,
    wu_ref,
    wv_ref,
    ecol_ref,
    erow_ref,
    mixed_ref,
    gg_ref,
    gu_ref,
    gv_ref,
    TS,
    XB,
    WS,
    WB,
    VT,
    GS,
    PB,
    RX,
    YP,
    YQ,
    YS,
    YR,
    HB,
    DD,
    ACC,
    OUT,
    MF,
    MB,
    MR,
    SS,
    SB,
    SL,
    SE,
    FS,
    FB,
    GO,
    GR,
    PT,
    x_send,
    x_recv,
    z_send,
    z_recv,
    s_send,
    s_recv,
    w_send,
    w_recv,
    p_send,
    p_recv,
    q_send,
    q_recv,
    y_send,
    y_recv,
    h_send,
    h_recv,
    m_send,
    m_recv,
    r_send,
    r_recv,
    f_send,
    f_recv,
    g_send,
    g_recv,
):
    E = Z * NX
    R = GROUP * E
    NH = Z // 2
    PAIRS = E // 2
    HALF = 2 * LANE
    dp = lax.axis_index("dp")
    ex = lax.axis_index("expert")
    y, c = dp // 2, dp % 2
    z, x = ex // NX, ex % NX
    other = 1 - c
    side = x // 2

    def dev(zz, xx, yy, cc):
        return (yy * 2 + cc, zz * NX + xx)

    z_next = dev((z + 1) % Z, x, y, c)
    z_prev = dev((z + Z - 1) % Z, x, y, c)
    sibling = dev(z, x, y, other)

    def remote(src, dst, send, recv, target):
        return pltpu.make_async_remote_copy(
            src_ref=src,
            dst_ref=dst,
            send_sem=send,
            recv_sem=recv,
            device_id=target,
            device_id_type=pl.DeviceIdType.MESH,
        )

    def wait_for(ref, sem):
        pltpu.make_async_copy(ref, ref, sem).wait()

    barrier = pltpu.get_barrier_semaphore()
    greeted = [z_next, z_prev]
    for dx in range(NX):
        for dc in range(2):
            if dx or dc:
                greeted.append(dev(z, (x + dx) % NX, y, (c + dc) % 2))
    for dy in range(1, Y):
        greeted.append(dev(z, x, (y + dy) % Y, c))
    for g in greeted:
        pl.semaphore_signal(barrier, inc=1, device_id=g, device_id_type=pl.DeviceIdType.MESH)

    for b in range(NX):
        lanes = slice(b * LANE, (b + 1) * LANE)
        TS[b, 0:LANE, :] = tok_ref[:, lanes]
        TS[b, LANE : LANE + META, :] = meta_ref[...]
        TS[b, LANE + META : BLK, :] = cot_ref[:, lanes]
    XB[0, x, c] = TS[x]
    pl.semaphore_wait(barrier, len(greeted))

    for dx in range(1, NX):
        to = (x + dx) % NX
        remote(
            TS.at[to], XB.at[0, x, c], x_send, x_recv.at[dx - 1], dev(z, to, y, c)
        ).start()

    ecol, erow = ecol_ref[...], erow_ref[...]
    same = ecol == erow
    i0 = lax.broadcasted_iota(jnp.int32, (R, R), 0)
    i1 = lax.broadcasted_iota(jnp.int32, (R, R), 1)
    rank_row = jnp.sum(jnp.where(same & (i0 < i1), 1.0, 0.0), axis=0, keepdims=True)
    rank_col = jnp.sum(jnp.where(same & (i1 < i0), 1.0, 0.0), axis=1, keepdims=True)
    pos_row = erow * GROUP + rank_row.astype(jnp.int32)
    pos_col = ecol * GROUP + rank_col.astype(jnp.int32)
    perm = jnp.where(i0 == pos_row, 1.0, 0.0).astype(BF)
    PT[...] = jnp.where(i1 == pos_col, 1.0, 0.0).astype(BF)
    def forward(s, tau):
        remote(
            XB.at[s, tau, c],
            XB.at[s + 1, tau, c],
            z_send.at[s],
            z_recv.at[s + 1, tau],
            z_next if tau < 2 else z_prev,
        ).start()

    def share(s, tau):
        remote(XB.at[s, tau, c], XB.at[s, tau, c], s_send.at[s], s_recv.at[s], sibling).start()

    for dx in range(1, NX):
        wait_for(XB.at[0, (x + NX - dx) % NX, c], x_recv.at[dx - 1])
    for tau in (0, 2, 1, 3):
        forward(0, tau)
    for tau in range(NX):
        share(0, tau)

    def arrive(s):
        for tau in (0, 2, 1, 3):
            wait_for(XB.at[s, tau, c], z_recv.at[s, tau])

            @pl.when(s < Z - 1)
            def _():
                forward(s, tau)

            share(s, tau)

    for a, w_ref in enumerate((wg_ref, wu_ref, wv_ref)):
        for b in range(NX):
            lanes = slice(b * LANE, (b + 1) * LANE)
            WS[a, b] = jnp.dot(perm, w_ref[:, lanes], preferred_element_type=F32).astype(BF)
        for dx in range(NX):
            to = (x + dx) % NX
            copy = remote(
                WS.at[a, to],
                WB.at[a, x % 2, c],
                w_send.at[a, dx],
                w_recv.at[a, x % 2, c],
                dev(z, to, y, side),
            )
            if dx:
                copy.start()
            else:

                @pl.when(c == side)
                def _():
                    WB[a, x % 2, c] = WS[a, x]

                @pl.when(c != side)
                def _():
                    copy.start()

    ACC[...] = jnp.zeros_like(ACC)
    for way in range(2):
        for half in range(2):
            first = NH if way == half else NH - 1
            SB[way, half, first] = jnp.zeros((LANE, HALF), BF)

    arrive(1)

    for a in range(3):
        for i in range(2):
            for cc in range(2):

                @pl.when(jnp.logical_not((2 * c + i == x) & (cc == c)))
                def _():
                    wait_for(WB.at[a, i, cc], w_recv.at[a, i, cc])

    for i in range(2):
        for cc in range(2):
            VT[cc * LANE : (cc + 1) * LANE, i * R : (i + 1) * R] = jnp.transpose(
                WB[2, i, cc].astype(F32)
            ).astype(BF)

    sub = lax.broadcasted_iota(jnp.int32, (16, LANE), 0) // 8

    def named(s, tau):
        rows = XB[s, tau, c, LANE : LANE + META, :].astype(F32)
        return [jnp.broadcast_to(rows[k : k + 1, :], (16, LANE)) for k in range(2)]

    def project(s):
        wait_for(XB.at[s, :, other], s_recv.at[s])
        for h in range(2):
            taus = (2 * h, 2 * h + 1)

            def rows_of(first):
                return jnp.concatenate(
                    [
                        jnp.concatenate(
                            [XB[s, tau, cc, first : first + LANE, :] for cc in range(2)], axis=1
                        )
                        for tau in taus
                    ],
                    axis=0,
                )

            for first, arrays in ((0, (0, 1)), (LANE + META, (2,))):
                right = rows_of(first)
                for a in arrays:
                    for i in range(2):
                        left = jnp.concatenate([WB[a, i, 0], WB[a, i, 1]], axis=1)
                        GS[a * 2 + i] = lax.dot_general(
                            left,
                            right,
                            (((1,), (1,)), ((), ())),
                            preferred_element_type=F32,
                        )
            for p, tau in enumerate(taus):
                lanes = slice(p * LANE, (p + 1) * LANE)
                who = [w[0:8] for w in named(s, tau)]
                kept = [[jnp.zeros((8, LANE), F32) for _ in range(6)] for _ in range(2)]
                for e in range(E):
                    hits = [who[k] == float(e) for k in range(2)]
                    for q in range(6):
                        value = GS[q, 8 * e : 8 * e + 8, lanes]
                        for k in range(2):
                            kept[k][q] = jnp.where(hits[k], value, kept[k][q])
                for a in range(3):
                    for k in range(2):
                        for i in range(2):
                            row = a * 32 + k * 16 + i * 8
                            PB[s, tau, row : row + 8, :] = kept[k][a * 2 + i]
        for dx in range(1, NX):
            to = (x + dx) % NX
            remote(
                PB.at[s, to], RX.at[s, dx - 1], p_send.at[s], p_recv.at[s], dev(z, to, y, c)
            ).start()

    def sum_x(s):
        wait_for(RX.at[s], p_recv.at[s])
        YP[s] = PB[s, x] + RX[s, 0] + RX[s, 1] + RX[s, 2]
        remote(
            YP.at[s], YQ.at[s], q_send.at[s], q_recv.at[s], dev(z, x, y + 1 - 2 * (y % 2), c)
        ).start()

    def sum_pair(s):
        wait_for(YQ.at[s], q_recv.at[s])
        YS[s] = (YP[s] + YQ[s]).astype(BF)
        for pair in range(1, Y // 2):
            remote(
                YS.at[s],
                YR.at[s, pair - 1],
                y_send.at[s],
                y_recv.at[s],
                dev(z, x, (y + 2 * pair) % Y, c),
            ).start()

    def activate(s):
        wait_for(YR.at[s], y_recv.at[s])
        total = YP[s] + YQ[s]
        for slot in range(Y // 2 - 1):
            total = total + YR[s, slot].astype(F32)
        meta = XB[s, x, c, LANE : LANE + META, :].astype(F32)
        for k in range(2):
            w = meta[2 + 3 * k : 3 + 3 * k] + meta[3 + 3 * k : 4 + 3 * k] + meta[4 + 3 * k : 5 + 3 * k]
            gate = total[k * 16 : k * 16 + 16]
            up = total[32 + k * 16 : 48 + k * 16]
            back = total[64 + k * 16 : 80 + k * 16] * w
            sig = 1.0 / (1.0 + jnp.exp(-gate))
            HB[s, x, k * 16 : k * 16 + 16, :] = (
                back * up * sig * (1.0 + gate * (1.0 - sig))
            ).astype(BF)
            HB[s, x, 32 + k * 16 : 48 + k * 16, :] = (back * gate * sig).astype(BF)
            HB[s, x, 64 + k * 16 : 80 + k * 16, :] = (w * (gate * sig * up)).astype(BF)
        for dx in range(1, NX):
            remote(
                HB.at[s, x], HB.at[s, x], h_send.at[s], h_recv.at[s, x], dev(z, (x + dx) % NX, y, c)
            ).start()

    def apply(s):
        for tau in range(NX):

            @pl.when(tau != x)
            def _():
                wait_for(HB.at[s, tau], h_recv.at[s, tau])

        for tau in range(NX):
            lanes = slice(tau * LANE, (tau + 1) * LANE)
            who = [(w - sub.astype(F32)).astype(BF) for w in named(s, tau)]
            twice = []
            for a in range(3):
                for k in range(2):
                    v = HB[s, tau, a * 32 + k * 16 : a * 32 + k * 16 + 16, :].astype(F32)
                    for i in range(2):
                        v8 = v[8 * i : 8 * i + 8]
                        twice.append(jnp.concatenate([v8, v8], axis=0).astype(BF))
            zero = jnp.zeros((16, LANE), BF)
            for m in range(PAIRS):
                hits = [who[k] == jnp.asarray(2 * m, BF) for k in range(2)]
                for a in range(3):
                    for i in range(2):
                        DD[a, i * R + 16 * m : i * R + 16 * m + 16, lanes] = jnp.where(
                            hits[0],
                            twice[a * 4 + i],
                            jnp.where(hits[1], twice[a * 4 + 2 + i], zero),
                        )
        out = jnp.dot(VT[...], DD[2], preferred_element_type=F32)
        OUT[0] = out[0:LANE]
        OUT[1] = out[LANE : 2 * LANE]
        MB[s] = OUT[other].astype(BF)
        remote(MB.at[s], MR.at[s], m_send.at[s], m_recv.at[s], sibling).start()
        MF[s] = OUT[c]
        for first, arrays in ((0, (0, 1)), (LANE + META, (2,))):
            right = jnp.concatenate(
                [
                    jnp.concatenate(
                        [XB[s, tau, cc, first : first + LANE, :] for cc in range(2)], axis=1
                    )
                    for tau in range(NX)
                ],
                axis=0,
            )
            for a in arrays:
                ACC[a] += jnp.dot(DD[a], right, preferred_element_type=F32)

    def own_output(s, half):
        lanes = slice(half * HALF, (half + 1) * HALF)
        return MF[s, :, lanes] + MR[s, :, lanes].astype(F32)

    def pass_on(d):
        def flow(way, half):
            first = NH if way == half else NH - 1

            @pl.when(d < first)
            def _():
                wait_for(SB.at[way, half, d], r_recv.at[way, half, d])

            s = d if way == half else Z - d
            total = own_output(s, half) + SB[way, half, d].astype(F32)

            @pl.when(d == 1)
            def _():
                SL[way, half] = total
                remote(
                    SL.at[way, half],
                    SE.at[way, half],
                    r_send.at[way, half, 1],
                    r_recv.at[way, half, 0],
                    z_prev if way == 0 else z_next,
                ).start()

            @pl.when(d > 1)
            def _():
                SS[way, half, d] = total.astype(BF)
                remote(
                    SS.at[way, half, d],
                    SB.at[way, half, d - 1],
                    r_send.at[way, half, d],
                    r_recv.at[way, half, d - 1],
                    z_prev if way == 0 else z_next,
                ).start()

        flow(0, 0)
        flow(1, 1)

        @pl.when(d < NH)
        def _():
            flow(0, 1)
            flow(1, 0)

    def step(it, carry):
        @pl.when(it < Z - 1)
        def _():
            arrive(it + 1)

        @pl.when((it >= 1) & (it < Z + 1))
        def _():
            project(it - 1)

        @pl.when((it >= 2) & (it < Z + 2))
        def _():
            sum_x(it - 2)

        @pl.when((it >= 3) & (it < Z + 3))
        def _():
            sum_pair(it - 3)

        @pl.when((it >= 4) & (it < Z + 4))
        def _():
            activate(it - 4)

        @pl.when(it >= 6 + NH)
        def _():
            s = it - 6
            wait_for(MR.at[s], m_recv.at[s])

            @pl.when(s > NH)
            def _():
                wait_for(MR.at[Z - s], m_recv.at[Z - s])

            pass_on(Z - s)

        @pl.when(it >= 5)
        def _():
            apply(it - 5)

        return carry

    lax.fori_loop(1, Z + 5, step, 0)

    for a in range(3):
        for i in range(2):
            for cc in range(2):
                GO[a, i, cc] = ACC[a, i * R : (i + 1) * R, cc * LANE : (cc + 1) * LANE].astype(BF)
        for i in range(2):
            for cc in range(2):
                mine = (2 * c + i == x) & (cc == c)

                @pl.when(jnp.logical_not(mine))
                def _():
                    remote(
                        GO.at[a, i, cc],
                        GR.at[a, x],
                        g_send.at[a, i, cc],
                        g_recv.at[a, x],
                        dev(z, 2 * c + i, y, cc),
                    ).start()

                @pl.when(mine)
                def _():
                    GR[a, x] = GO[a, i, cc]

    wait_for(MR.at[Z - 1], m_recv.at[Z - 1])
    wait_for(MR.at[1], m_recv.at[1])
    pass_on(1)

    wait_for(MR.at[0], m_recv.at[0])
    for way in range(2):
        for half in range(2):
            wait_for(SE.at[way, half], r_recv.at[way, half, 0])
    for half in range(2):
        done = (
            own_output(0, half) + SE[0, half] + SE[1, half]
        ).astype(BF)
        for p in range(2):
            FS[2 * half + p] = done[:, p * LANE : (p + 1) * LANE]
    for dx in range(1, NX):
        to = (x + dx) % NX
        remote(FS.at[to], FB.at[x], f_send.at[dx - 1], f_recv.at[dx - 1], dev(z, to, y, c)).start()
    FB[x] = FS[x]
    for dx in range(1, NX):
        wait_for(FB.at[(x + NX - dx) % NX], f_recv.at[dx - 1])
    for b in range(NX):
        mixed_ref[:, b * LANE : (b + 1) * LANE] = jnp.transpose(FB[b].astype(F32)).astype(BF)

    for a, out_ref in enumerate((gg_ref, gu_ref, gv_ref)):
        for dx in range(NX):
            frm = (x + dx) % NX
            if dx:
                wait_for(GR.at[a, frm], g_recv.at[a, frm])
            else:

                @pl.when(c != side)
                def _():
                    wait_for(GR.at[a, frm], g_recv.at[a, frm])

        for b in range(NX):
            out_ref[:, b * LANE : (b + 1) * LANE] = jnp.dot(
                PT[...], GR[a, b], preferred_element_type=F32
            ).astype(BF)

    wait_for(TS.at[0 : NX - 1], x_send)
    for s in range(Z):
        if s < Z - 1:
            wait_for(XB.at[s, :, c], z_send.at[s])
        wait_for(XB.at[s, :, c], s_send.at[s])
        wait_for(MR.at[s], m_send.at[s])
        wait_for(RX.at[s], p_send.at[s])
        wait_for(YR.at[s], y_send.at[s])
        wait_for(YQ.at[s], q_send.at[s])
        wait_for(HB.at[s, 0 : NX - 1], h_send.at[s])
    for a in range(3):
        for dx in range(NX):
            if dx:
                wait_for(WS.at[a, 0], w_send.at[a, dx])
            else:

                @pl.when(c != side)
                def _():
                    wait_for(WS.at[a, 0], w_send.at[a, 0])

        for i in range(2):
            for cc in range(2):

                @pl.when(jnp.logical_not((2 * c + i == x) & (cc == c)))
                def _():
                    wait_for(GO.at[a, i, cc], g_send.at[a, i, cc])

    for dx in range(1, NX):
        wait_for(FS.at[0], f_send.at[dx - 1])
    for way in range(2):
        for half in range(2):
            first = NH if way == half else NH - 1
            wait_for(SL.at[way, half], r_send.at[way, half, 1])
            for d in range(2, first + 1):
                wait_for(SS.at[way, half, d], r_send.at[way, half, d])


def local(Z, Y, tokens, cotangent, routes, route_weight, gate_dense, up_dense, down_dense, slice_map):
    rows, width = gate_dense.shape
    E = Z * NX
    here = lax.axis_index("expert")
    own = lax.dynamic_slice_in_dim(slice_map, here * rows, rows) // rows
    high = lax.reduce_precision(route_weight, 8, 7)
    rest = route_weight - high
    mid = lax.reduce_precision(rest, 8, 7)
    low = rest - mid
    pieces = [routes.astype(F32)] + [
        jnp.stack([high[:, k], mid[:, k], low[:, k]], axis=1) for k in range(2)
    ]
    meta = jnp.concatenate(pieces + [jnp.zeros((LANE, META - 8), F32)], axis=1).T.astype(BF)
    dma = pltpu.SemaphoreType.DMA
    NH = Z // 2
    scratch = [
        pltpu.VMEM((NX, BLK, LANE), BF),
        pltpu.VMEM((Z, NX, 2, BLK, LANE), BF),
        pltpu.VMEM((3, NX, rows, LANE), BF),
        pltpu.VMEM((3, 2, 2, rows, LANE), BF),
        pltpu.VMEM((2 * LANE, 2 * rows), BF),
        pltpu.VMEM((6, rows, 2 * LANE), F32),
        pltpu.VMEM((Z, NX, 96, LANE), F32),
        pltpu.VMEM((Z, NX - 1, 96, LANE), F32),
        pltpu.VMEM((Z, 96, LANE), F32),
        pltpu.VMEM((Z, 96, LANE), F32),
        pltpu.VMEM((Z, 96, LANE), BF),
        pltpu.VMEM((Z, Y // 2 - 1, 96, LANE), BF),
        pltpu.VMEM((Z, NX, 96, LANE), BF),
        pltpu.VMEM((3, 2 * rows, 4 * LANE), BF),
        pltpu.VMEM((3, 2 * rows, 2 * LANE), F32),
        pltpu.VMEM((2, LANE, 4 * LANE), F32),
        pltpu.VMEM((Z, LANE, 4 * LANE), F32),
        pltpu.VMEM((Z, LANE, 4 * LANE), BF),
        pltpu.VMEM((Z, LANE, 4 * LANE), BF),
        pltpu.VMEM((2, 2, NH + 1, LANE, 2 * LANE), BF),
        pltpu.VMEM((2, 2, NH + 1, LANE, 2 * LANE), BF),
        pltpu.VMEM((2, 2, LANE, 2 * LANE), F32),
        pltpu.VMEM((2, 2, LANE, 2 * LANE), F32),
        pltpu.VMEM((NX, LANE, LANE), BF),
        pltpu.VMEM((NX, LANE, LANE), BF),
        pltpu.VMEM((3, 2, 2, rows, LANE), BF),
        pltpu.VMEM((3, NX, rows, LANE), BF),
        pltpu.VMEM((rows, rows), BF),
        dma,
        dma((NX - 1,)),
        dma((Z,)),
        dma((Z, NX)),
        dma((Z,)),
        dma((Z,)),
        dma((3, NX)),
        dma((3, 2, 2)),
        dma((Z,)),
        dma((Z,)),
        dma((Z,)),
        dma((Z,)),
        dma((Z,)),
        dma((Z,)),
        dma((Z,)),
        dma((Z, NX)),
        dma((Z,)),
        dma((Z,)),
        dma((2, 2, NH + 1)),
        dma((2, 2, NH + 1)),
        dma((NX - 1,)),
        dma((NX - 1,)),
        dma((3, 2, 2)),
        dma((3, NX)),
    ]
    vmem = pl.BlockSpec(memory_space=pltpu.VMEM)
    return pl.pallas_call(
        functools.partial(layer_kernel, Z, Y),
        out_shape=(
            jax.ShapeDtypeStruct(tokens.shape, BF),
            jax.ShapeDtypeStruct(gate_dense.shape, BF),
            jax.ShapeDtypeStruct(gate_dense.shape, BF),
            jax.ShapeDtypeStruct(gate_dense.shape, BF),
        ),
        in_specs=[vmem] * 8,
        out_specs=(vmem,) * 4,
        scratch_shapes=scratch,
        compiler_params=pltpu.CompilerParams(
            collective_id=0, has_side_effects=True, vmem_limit_bytes=52 * 1024 * 1024
        ),
    )(
        meta,
        tokens,
        cotangent,
        gate_dense,
        up_dense,
        down_dense,
        own.reshape(rows, 1),
        own.reshape(1, rows),
    )


def solution(mesh):
    Y = mesh.shape["dp"] // 2
    Z = mesh.shape["expert"] // NX
    return jax.shard_map(
        functools.partial(local, Z, Y),
        mesh=mesh,
        in_specs=(
            P("expert", "dp"),
            P("expert", "dp"),
            P("expert", None),
            P("expert", None),
            P("expert", "dp"),
            P("expert", "dp"),
            P("expert", "dp"),
            P(),
        ),
        out_specs=(P("expert", "dp"), P("expert", "dp"), P("expert", "dp"), P("expert", "dp")),
        check_vma=False,
    )
```

```python
import functools

import jax
import jax.numpy as jnp
from jax import lax
from jax.experimental import pallas as pl
from jax.experimental.pallas import tpu as pltpu
from jax.sharding import PartitionSpec as P

BF = jnp.bfloat16
F32 = jnp.float32
NX = 4
LANE = 128
META = 16
BLK = 2 * LANE + META
GROUP = 8


def layer_kernel(
    Z,
    Y,
    meta_ref,
    tok_ref,
    cot_ref,
    wg_ref,
    wu_ref,
    wv_ref,
    ecol_ref,
    erow_ref,
    mixed_ref,
    gg_ref,
    gu_ref,
    gv_ref,
    TS,
    XB,
    WS,
    WB,
    VT,
    GS,
    PB,
    RX,
    YP,
    YQ,
    YS,
    YR,
    HB,
    DD,
    ACC,
    OUT,
    MF,
    MB,
    MR,
    SS,
    SB,
    SL,
    SE,
    FS,
    FB,
    GO,
    GR,
    PT,
    x_send,
    x_recv,
    z_send,
    z_recv,
    s_send,
    s_recv,
    w_send,
    w_recv,
    p_send,
    p_recv,
    q_send,
    q_recv,
    y_send,
    y_recv,
    h_send,
    h_recv,
    m_send,
    m_recv,
    r_send,
    r_recv,
    f_send,
    f_recv,
    g_send,
    g_recv,
):
    E = Z * NX
    R = GROUP * E
    NH = Z // 2
    PAIRS = E // 2
    HALF = 2 * LANE
    dp = lax.axis_index("dp")
    ex = lax.axis_index("expert")
    y, c = dp // 2, dp % 2
    z, x = ex // NX, ex % NX
    other = 1 - c
    side = x // 2

    def dev(zz, xx, yy, cc):
        return (yy * 2 + cc, zz * NX + xx)

    z_next = dev((z + 1) % Z, x, y, c)
    z_prev = dev((z + Z - 1) % Z, x, y, c)
    sibling = dev(z, x, y, other)

    def remote(src, dst, send, recv, target):
        return pltpu.make_async_remote_copy(
            src_ref=src,
            dst_ref=dst,
            send_sem=send,
            recv_sem=recv,
            device_id=target,
            device_id_type=pl.DeviceIdType.MESH,
        )

    def wait_for(ref, sem):
        pltpu.make_async_copy(ref, ref, sem).wait()

    barrier = pltpu.get_barrier_semaphore()
    greeted = [z_next, z_prev]
    for dx in range(NX):
        for dc in range(2):
            if dx or dc:
                greeted.append(dev(z, (x + dx) % NX, y, (c + dc) % 2))
    for dy in range(1, Y):
        greeted.append(dev(z, x, (y + dy) % Y, c))
    for g in greeted:
        pl.semaphore_signal(barrier, inc=1, device_id=g, device_id_type=pl.DeviceIdType.MESH)

    for b in range(NX):
        lanes = slice(b * LANE, (b + 1) * LANE)
        TS[b, 0:LANE, :] = tok_ref[:, lanes]
        TS[b, LANE : LANE + META, :] = meta_ref[...]
        TS[b, LANE + META : BLK, :] = cot_ref[:, lanes]
    XB[0, x, c] = TS[x]
    pl.semaphore_wait(barrier, len(greeted))

    for dx in range(1, NX):
        to = (x + dx) % NX
        remote(
            TS.at[to], XB.at[0, x, c], x_send, x_recv.at[dx - 1], dev(z, to, y, c)
        ).start()

    ecol, erow = ecol_ref[...], erow_ref[...]
    same = ecol == erow
    i0 = lax.broadcasted_iota(jnp.int32, (R, R), 0)
    i1 = lax.broadcasted_iota(jnp.int32, (R, R), 1)
    rank_row = jnp.sum(jnp.where(same & (i0 < i1), 1.0, 0.0), axis=0, keepdims=True)
    rank_col = jnp.sum(jnp.where(same & (i1 < i0), 1.0, 0.0), axis=1, keepdims=True)
    pos_row = erow * GROUP + rank_row.astype(jnp.int32)
    pos_col = ecol * GROUP + rank_col.astype(jnp.int32)
    perm = jnp.where(i0 == pos_row, 1.0, 0.0).astype(BF)
    PT[...] = jnp.where(i1 == pos_col, 1.0, 0.0).astype(BF)
    def forward(s, tau):
        remote(
            XB.at[s, tau, c],
            XB.at[s + 1, tau, c],
            z_send.at[s],
            z_recv.at[s + 1, tau],
            z_next if tau < 2 else z_prev,
        ).start()

    def share(s, tau):
        remote(XB.at[s, tau, c], XB.at[s, tau, c], s_send.at[s], s_recv.at[s], sibling).start()

    for dx in range(1, NX):
        wait_for(XB.at[0, (x + NX - dx) % NX, c], x_recv.at[dx - 1])
    for tau in (0, 2, 1, 3):
        forward(0, tau)
    for tau in range(NX):
        share(0, tau)

    def arrive(s):
        for tau in (0, 2, 1, 3):
            wait_for(XB.at[s, tau, c], z_recv.at[s, tau])

            @pl.when(s < Z - 1)
            def _():
                forward(s, tau)

            share(s, tau)

    for a, w_ref in enumerate((wg_ref, wu_ref, wv_ref)):
        for b in range(NX):
            lanes = slice(b * LANE, (b + 1) * LANE)
            WS[a, b] = jnp.dot(perm, w_ref[:, lanes], preferred_element_type=F32).astype(BF)
        for dx in range(NX):
            to = (x + dx) % NX
            copy = remote(
                WS.at[a, to],
                WB.at[a, x % 2, c],
                w_send.at[a, dx],
                w_recv.at[a, x % 2, c],
                dev(z, to, y, side),
            )
            if dx:
                copy.start()
            else:

                @pl.when(c == side)
                def _():
                    WB[a, x % 2, c] = WS[a, x]

                @pl.when(c != side)
                def _():
                    copy.start()

    ACC[...] = jnp.zeros_like(ACC)
    for way in range(2):
        for half in range(2):
            first = NH if way == half else NH - 1
            SB[way, half, first] = jnp.zeros((LANE, HALF), BF)

    for s in range(1, 4):
        arrive(s)

    for a in range(3):
        for i in range(2):
            for cc in range(2):

                @pl.when(jnp.logical_not((2 * c + i == x) & (cc == c)))
                def _():
                    wait_for(WB.at[a, i, cc], w_recv.at[a, i, cc])

    for i in range(2):
        for cc in range(2):
            VT[cc * LANE : (cc + 1) * LANE, i * R : (i + 1) * R] = jnp.transpose(
                WB[2, i, cc].astype(F32)
            ).astype(BF)

    sub = lax.broadcasted_iota(jnp.int32, (16, LANE), 0) // 8

    def named(s, tau):
        rows = XB[s, tau, c, LANE : LANE + META, :].astype(F32)
        return [jnp.broadcast_to(rows[k : k + 1, :], (16, LANE)) for k in range(2)]

    def project(s):
        wait_for(XB.at[s, :, other], s_recv.at[s])
        for h in range(2):
            taus = (2 * h, 2 * h + 1)

            def rows_of(first):
                return jnp.concatenate(
                    [
                        jnp.concatenate(
                            [XB[s, tau, cc, first : first + LANE, :] for cc in range(2)], axis=1
                        )
                        for tau in taus
                    ],
                    axis=0,
                )

            for first, arrays in ((0, (0, 1)), (LANE + META, (2,))):
                right = rows_of(first)
                for a in arrays:
                    for i in range(2):
                        left = jnp.concatenate([WB[a, i, 0], WB[a, i, 1]], axis=1)
                        GS[a * 2 + i] = lax.dot_general(
                            left,
                            right,
                            (((1,), (1,)), ((), ())),
                            preferred_element_type=F32,
                        )
            for p, tau in enumerate(taus):
                lanes = slice(p * LANE, (p + 1) * LANE)
                who = [w[0:8] for w in named(s, tau)]
                kept = [[jnp.zeros((8, LANE), F32) for _ in range(6)] for _ in range(2)]
                for e in range(E):
                    hits = [who[k] == float(e) for k in range(2)]
                    for q in range(6):
                        value = GS[q, 8 * e : 8 * e + 8, lanes]
                        for k in range(2):
                            kept[k][q] = jnp.where(hits[k], value, kept[k][q])
                for a in range(3):
                    for k in range(2):
                        for i in range(2):
                            row = a * 32 + k * 16 + i * 8
                            PB[s, tau, row : row + 8, :] = kept[k][a * 2 + i]
        for dx in range(1, NX):
            to = (x + dx) % NX
            remote(
                PB.at[s, to], RX.at[s, dx - 1], p_send.at[s], p_recv.at[s], dev(z, to, y, c)
            ).start()

    def sum_x(s):
        wait_for(RX.at[s], p_recv.at[s])
        YP[s] = PB[s, x] + RX[s, 0] + RX[s, 1] + RX[s, 2]
        remote(
            YP.at[s], YQ.at[s], q_send.at[s], q_recv.at[s], dev(z, x, y + 1 - 2 * (y % 2), c)
        ).start()

    def sum_pair(s):
        wait_for(YQ.at[s], q_recv.at[s])
        YS[s] = (YP[s] + YQ[s]).astype(BF)
        for pair in range(1, Y // 2):
            remote(
                YS.at[s],
                YR.at[s, pair - 1],
                y_send.at[s],
                y_recv.at[s],
                dev(z, x, (y + 2 * pair) % Y, c),
            ).start()

    def activate(s):
        wait_for(YR.at[s], y_recv.at[s])
        total = YP[s] + YQ[s]
        for slot in range(Y // 2 - 1):
            total = total + YR[s, slot].astype(F32)
        meta = XB[s, x, c, LANE : LANE + META, :].astype(F32)
        for k in range(2):
            w = meta[2 + 3 * k : 3 + 3 * k] + meta[3 + 3 * k : 4 + 3 * k] + meta[4 + 3 * k : 5 + 3 * k]
            gate = total[k * 16 : k * 16 + 16]
            up = total[32 + k * 16 : 48 + k * 16]
            back = total[64 + k * 16 : 80 + k * 16] * w
            sig = 1.0 / (1.0 + jnp.exp(-gate))
            HB[s, x, k * 16 : k * 16 + 16, :] = (
                back * up * sig * (1.0 + gate * (1.0 - sig))
            ).astype(BF)
            HB[s, x, 32 + k * 16 : 48 + k * 16, :] = (back * gate * sig).astype(BF)
            HB[s, x, 64 + k * 16 : 80 + k * 16, :] = (w * (gate * sig * up)).astype(BF)
        for dx in range(1, NX):
            remote(
                HB.at[s, x], HB.at[s, x], h_send.at[s], h_recv.at[s, x], dev(z, (x + dx) % NX, y, c)
            ).start()

    def apply(s):
        for tau in range(NX):

            @pl.when(tau != x)
            def _():
                wait_for(HB.at[s, tau], h_recv.at[s, tau])

        for tau in range(NX):
            lanes = slice(tau * LANE, (tau + 1) * LANE)
            who = [(w - sub.astype(F32)).astype(BF) for w in named(s, tau)]
            twice = []
            for a in range(3):
                for k in range(2):
                    v = HB[s, tau, a * 32 + k * 16 : a * 32 + k * 16 + 16, :].astype(F32)
                    for i in range(2):
                        v8 = v[8 * i : 8 * i + 8]
                        twice.append(jnp.concatenate([v8, v8], axis=0).astype(BF))
            zero = jnp.zeros((16, LANE), BF)
            for m in range(PAIRS):
                hits = [who[k] == jnp.asarray(2 * m, BF) for k in range(2)]
                for a in range(3):
                    for i in range(2):
                        DD[a, i * R + 16 * m : i * R + 16 * m + 16, lanes] = jnp.where(
                            hits[0],
                            twice[a * 4 + i],
                            jnp.where(hits[1], twice[a * 4 + 2 + i], zero),
                        )
        out = jnp.dot(VT[...], DD[2], preferred_element_type=F32)
        OUT[0] = out[0:LANE]
        OUT[1] = out[LANE : 2 * LANE]
        MB[s] = OUT[other].astype(BF)
        remote(MB.at[s], MR.at[s], m_send.at[s], m_recv.at[s], sibling).start()
        MF[s] = OUT[c]
        for first, arrays in ((0, (0, 1)), (LANE + META, (2,))):
            right = jnp.concatenate(
                [
                    jnp.concatenate(
                        [XB[s, tau, cc, first : first + LANE, :] for cc in range(2)], axis=1
                    )
                    for tau in range(NX)
                ],
                axis=0,
            )
            for a in arrays:
                ACC[a] += jnp.dot(DD[a], right, preferred_element_type=F32)

    def own_output(s, half):
        lanes = slice(half * HALF, (half + 1) * HALF)
        return MF[s, :, lanes] + MR[s, :, lanes].astype(F32)

    def pass_on(d):
        def flow(way, half):
            first = NH if way == half else NH - 1

            @pl.when(d < first)
            def _():
                wait_for(SB.at[way, half, d], r_recv.at[way, half, d])

            s = d if way == half else Z - d
            total = own_output(s, half) + SB[way, half, d].astype(F32)

            @pl.when(d == 1)
            def _():
                SL[way, half] = total
                remote(
                    SL.at[way, half],
                    SE.at[way, half],
                    r_send.at[way, half, 1],
                    r_recv.at[way, half, 0],
                    z_prev if way == 0 else z_next,
                ).start()

            @pl.when(d > 1)
            def _():
                SS[way, half, d] = total.astype(BF)
                remote(
                    SS.at[way, half, d],
                    SB.at[way, half, d - 1],
                    r_send.at[way, half, d],
                    r_recv.at[way, half, d - 1],
                    z_prev if way == 0 else z_next,
                ).start()

        flow(0, 0)
        flow(1, 1)

        @pl.when(d < NH)
        def _():
            flow(0, 1)
            flow(1, 0)

    def step(it, carry):
        @pl.when(it < Z - 3)
        def _():
            arrive(it + 3)

        @pl.when((it >= 1) & (it < Z + 1))
        def _():
            project(it - 1)

        @pl.when((it >= 2) & (it < Z + 2))
        def _():
            sum_x(it - 2)

        @pl.when((it >= 3) & (it < Z + 3))
        def _():
            sum_pair(it - 3)

        @pl.when((it >= 4) & (it < Z + 4))
        def _():
            activate(it - 4)

        @pl.when(it >= 6 + NH)
        def _():
            s = it - 6
            wait_for(MR.at[s], m_recv.at[s])

            @pl.when(s > NH)
            def _():
                wait_for(MR.at[Z - s], m_recv.at[Z - s])

            pass_on(Z - s)

        @pl.when(it >= 5)
        def _():
            apply(it - 5)

        return carry

    lax.fori_loop(1, Z + 5, step, 0)

    for a in range(3):
        for i in range(2):
            for cc in range(2):
                GO[a, i, cc] = ACC[a, i * R : (i + 1) * R, cc * LANE : (cc + 1) * LANE].astype(BF)
        for i in range(2):
            for cc in range(2):
                mine = (2 * c + i == x) & (cc == c)

                @pl.when(jnp.logical_not(mine))
                def _():
                    remote(
                        GO.at[a, i, cc],
                        GR.at[a, x],
                        g_send.at[a, i, cc],
                        g_recv.at[a, x],
                        dev(z, 2 * c + i, y, cc),
                    ).start()

                @pl.when(mine)
                def _():
                    GR[a, x] = GO[a, i, cc]

    wait_for(MR.at[Z - 1], m_recv.at[Z - 1])
    wait_for(MR.at[1], m_recv.at[1])
    pass_on(1)

    wait_for(MR.at[0], m_recv.at[0])
    for way in range(2):
        for half in range(2):
            wait_for(SE.at[way, half], r_recv.at[way, half, 0])
    for half in range(2):
        done = (
            own_output(0, half) + SE[0, half] + SE[1, half]
        ).astype(BF)
        for p in range(2):
            FS[2 * half + p] = done[:, p * LANE : (p + 1) * LANE]
    for dx in range(1, NX):
        to = (x + dx) % NX
        remote(FS.at[to], FB.at[x], f_send.at[dx - 1], f_recv.at[dx - 1], dev(z, to, y, c)).start()
    FB[x] = FS[x]
    for dx in range(1, NX):
        wait_for(FB.at[(x + NX - dx) % NX], f_recv.at[dx - 1])
    for b in range(NX):
        mixed_ref[:, b * LANE : (b + 1) * LANE] = jnp.transpose(FB[b].astype(F32)).astype(BF)

    for a, out_ref in enumerate((gg_ref, gu_ref, gv_ref)):
        for dx in range(NX):
            frm = (x + dx) % NX
            if dx:
                wait_for(GR.at[a, frm], g_recv.at[a, frm])
            else:

                @pl.when(c != side)
                def _():
                    wait_for(GR.at[a, frm], g_recv.at[a, frm])

        for b in range(NX):
            out_ref[:, b * LANE : (b + 1) * LANE] = jnp.dot(
                PT[...], GR[a, b], preferred_element_type=F32
            ).astype(BF)

    wait_for(TS.at[0 : NX - 1], x_send)
    for s in range(Z):
        if s < Z - 1:
            wait_for(XB.at[s, :, c], z_send.at[s])
        wait_for(XB.at[s, :, c], s_send.at[s])
        wait_for(MR.at[s], m_send.at[s])
        wait_for(RX.at[s], p_send.at[s])
        wait_for(YR.at[s], y_send.at[s])
        wait_for(YQ.at[s], q_send.at[s])
        wait_for(HB.at[s, 0 : NX - 1], h_send.at[s])
    for a in range(3):
        for dx in range(NX):
            if dx:
                wait_for(WS.at[a, 0], w_send.at[a, dx])
            else:

                @pl.when(c != side)
                def _():
                    wait_for(WS.at[a, 0], w_send.at[a, 0])

        for i in range(2):
            for cc in range(2):

                @pl.when(jnp.logical_not((2 * c + i == x) & (cc == c)))
                def _():
                    wait_for(GO.at[a, i, cc], g_send.at[a, i, cc])

    for dx in range(1, NX):
        wait_for(FS.at[0], f_send.at[dx - 1])
    for way in range(2):
        for half in range(2):
            first = NH if way == half else NH - 1
            wait_for(SL.at[way, half], r_send.at[way, half, 1])
            for d in range(2, first + 1):
                wait_for(SS.at[way, half, d], r_send.at[way, half, d])


def local(Z, Y, tokens, cotangent, routes, route_weight, gate_dense, up_dense, down_dense, slice_map):
    rows, width = gate_dense.shape
    E = Z * NX
    here = lax.axis_index("expert")
    own = lax.dynamic_slice_in_dim(slice_map, here * rows, rows) // rows
    high = lax.reduce_precision(route_weight, 8, 7)
    rest = route_weight - high
    mid = lax.reduce_precision(rest, 8, 7)
    low = rest - mid
    pieces = [routes.astype(F32)] + [
        jnp.stack([high[:, k], mid[:, k], low[:, k]], axis=1) for k in range(2)
    ]
    meta = jnp.concatenate(pieces + [jnp.zeros((LANE, META - 8), F32)], axis=1).T.astype(BF)
    dma = pltpu.SemaphoreType.DMA
    NH = Z // 2
    scratch = [
        pltpu.VMEM((NX, BLK, LANE), BF),
        pltpu.VMEM((Z, NX, 2, BLK, LANE), BF),
        pltpu.VMEM((3, NX, rows, LANE), BF),
        pltpu.VMEM((3, 2, 2, rows, LANE), BF),
        pltpu.VMEM((2 * LANE, 2 * rows), BF),
        pltpu.VMEM((6, rows, 2 * LANE), F32),
        pltpu.VMEM((Z, NX, 96, LANE), F32),
        pltpu.VMEM((Z, NX - 1, 96, LANE), F32),
        pltpu.VMEM((Z, 96, LANE), F32),
        pltpu.VMEM((Z, 96, LANE), F32),
        pltpu.VMEM((Z, 96, LANE), BF),
        pltpu.VMEM((Z, Y // 2 - 1, 96, LANE), BF),
        pltpu.VMEM((Z, NX, 96, LANE), BF),
        pltpu.VMEM((3, 2 * rows, 4 * LANE), BF),
        pltpu.VMEM((3, 2 * rows, 2 * LANE), F32),
        pltpu.VMEM((2, LANE, 4 * LANE), F32),
        pltpu.VMEM((Z, LANE, 4 * LANE), F32),
        pltpu.VMEM((Z, LANE, 4 * LANE), BF),
        pltpu.VMEM((Z, LANE, 4 * LANE), BF),
        pltpu.VMEM((2, 2, NH + 1, LANE, 2 * LANE), BF),
        pltpu.VMEM((2, 2, NH + 1, LANE, 2 * LANE), BF),
        pltpu.VMEM((2, 2, LANE, 2 * LANE), F32),
        pltpu.VMEM((2, 2, LANE, 2 * LANE), F32),
        pltpu.VMEM((NX, LANE, LANE), BF),
        pltpu.VMEM((NX, LANE, LANE), BF),
        pltpu.VMEM((3, 2, 2, rows, LANE), BF),
        pltpu.VMEM((3, NX, rows, LANE), BF),
        pltpu.VMEM((rows, rows), BF),
        dma,
        dma((NX - 1,)),
        dma((Z,)),
        dma((Z, NX)),
        dma((Z,)),
        dma((Z,)),
        dma((3, NX)),
        dma((3, 2, 2)),
        dma((Z,)),
        dma((Z,)),
        dma((Z,)),
        dma((Z,)),
        dma((Z,)),
        dma((Z,)),
        dma((Z,)),
        dma((Z, NX)),
        dma((Z,)),
        dma((Z,)),
        dma((2, 2, NH + 1)),
        dma((2, 2, NH + 1)),
        dma((NX - 1,)),
        dma((NX - 1,)),
        dma((3, 2, 2)),
        dma((3, NX)),
    ]
    vmem = pl.BlockSpec(memory_space=pltpu.VMEM)
    return pl.pallas_call(
        functools.partial(layer_kernel, Z, Y),
        out_shape=(
            jax.ShapeDtypeStruct(tokens.shape, BF),
            jax.ShapeDtypeStruct(gate_dense.shape, BF),
            jax.ShapeDtypeStruct(gate_dense.shape, BF),
            jax.ShapeDtypeStruct(gate_dense.shape, BF),
        ),
        in_specs=[vmem] * 8,
        out_specs=(vmem,) * 4,
        scratch_shapes=scratch,
        compiler_params=pltpu.CompilerParams(
            collective_id=0, has_side_effects=True, vmem_limit_bytes=52 * 1024 * 1024
        ),
    )(
        meta,
        tokens,
        cotangent,
        gate_dense,
        up_dense,
        down_dense,
        own.reshape(rows, 1),
        own.reshape(1, rows),
    )


def solution(mesh):
    Y = mesh.shape["dp"] // 2
    Z = mesh.shape["expert"] // NX
    return jax.shard_map(
        functools.partial(local, Z, Y),
        mesh=mesh,
        in_specs=(
            P("expert", "dp"),
            P("expert", "dp"),
            P("expert", None),
            P("expert", None),
            P("expert", "dp"),
            P("expert", "dp"),
            P("expert", "dp"),
            P(),
        ),
        out_specs=(P("expert", "dp"), P("expert", "dp"), P("expert", "dp"), P("expert", "dp")),
        check_vma=False,
    )
```
